32 devices in a mesh: row: 4 (over x, core), col: 8 (over z, y).
Axes of the slice: x: 2, y: 2, z: 4, core: 2. Of those that a mesh axis runs over, the one named last changes fastest.
Arguments:
- sources: bfloat16 [4096, 768], P(('row', 'col')), may hold values from -2 to 2
- targets: bfloat16 [4096, 768], P(('col', 'row')), may hold values from -2 to 2
- projection: bfloat16 [768, 768], replicated, may hold values from -0.21875 to 0.21875
- language: int32 [4096], replicated, may hold values from 0 to 108
- lang_allow: int32 [109, 109], replicated, may hold values 0 or 1
- tile_allow: int32 [8, 8], replicated, may hold values 0 or 1
Outputs:
- grad_sources: bfloat16 [4096, 768], P(('row', 'col'))
- grad_targets: bfloat16 [4096, 768], P(('col', 'row'))
- grad_proj: float32 [768, 768], replicated
The draws below stay inside these ranges and needn't reach their ends.
All inputs are finite; a program needn't handle non-finite values.
Results may differ from the reference program's by a relative error of at most 0.0035.
The reference program's roundings to bfloat16 on the way (of `logit_grad`) count: a program that leaves them out, or rounds other values in their place, can miss the bound.
Values may be sent and summed in bfloat16 or wider, within the bound.
A program may use at most 128 MiB of HBM per device.

```python
import math
import jax
import jax.numpy as jnp
from jax import lax

D = 768
NL = 109
TILE = 512
PAIRS = 4096
NT = 8


def pair_parts(key):
    key_topic, key_centre, key_own, key_strength = jax.random.split(key, 4)
    topic_count = min(64, max(PAIRS // 8, 1))
    topic = jax.random.randint(key_topic, (PAIRS,), 0, topic_count)
    centres = jax.random.normal(key_centre, (topic_count, D), jnp.float32)
    own = jax.random.normal(key_own, (PAIRS, D), jnp.float32)
    strength = jax.random.uniform(key_strength, (PAIRS, 1), jnp.float32, 0.15, 0.85)
    base = strength * centres[topic]
    rest = jnp.sqrt(1.0 - strength * strength)
    return (base, own, rest)


def draw_sources(key, part):
    base, own, rest = pair_parts(key)
    values = base + rest * own
    values = jnp.clip(values * D ** (-0.5), -2.0, 2.0)
    return values.astype(jnp.bfloat16)


def draw_targets(key, part):
    own_key = jax.random.fold_in(key, 23)
    base, own, rest = pair_parts(key)
    noise_key = jax.random.fold_in(own_key, 0)
    noise = jax.random.normal(noise_key, (PAIRS, D), jnp.float32)
    values = base + rest * (0.92 * own + 0.39 * noise)
    values = jnp.clip(values * D ** (-0.5), -2.0, 2.0)
    return values.astype(jnp.bfloat16)


def touch_ends(entries, key, low, high):
    longest = entries.shape.index(max(entries.shape))
    spots = []
    for shift in (0, 1):
        where = [jax.random.randint(jax.random.fold_in(key, axis), (), 0, length) for axis, length in enumerate(entries.shape)]
        where[longest] = (where[longest] + shift) % entries.shape[longest]
        spots.append(tuple(where))
    return entries.at[spots[0]].set(low).at[spots[1]].set(high)


def normal_values(rng, extent, scale, limit, held_as=jnp.bfloat16):
    array = jax.random.normal(rng, extent, jnp.float32) * scale
    return jnp.minimum(jnp.maximum(array, -limit), limit).astype(held_as)


def setup_inputs(seed: int = 0) -> dict:
    arg_keys = jax.random.split(jax.random.key(seed), 7)
    sources = draw_sources(jax.random.fold_in(arg_keys[6], 71), 0)
    targets = draw_targets(jax.random.fold_in(arg_keys[6], 71), 0)
    projection = normal_values(arg_keys[2], (D, D), D ** -0.5, 0.21875)
    language = touch_ends(jax.random.randint(arg_keys[3], (PAIRS,), 0, NL), jax.random.fold_in(arg_keys[3], 1), 0, NL - 1).astype(jnp.int32)
    lang_allow = touch_ends((jax.random.randint(arg_keys[4], (NL, NL), 0, 4) < 3).astype(jnp.int32), jax.random.fold_in(arg_keys[4], 1), 0, 1)
    tile_allow = touch_ends((jax.random.randint(arg_keys[5], (NT, NT), 0, 2) < 1).astype(jnp.int32), jax.random.fold_in(arg_keys[5], 1), 0, 1)
    return {"sources": sources, "targets": targets, "projection": projection, "language": language, "lang_allow": lang_allow, "tile_allow": tile_allow}


SCALE = 20.0
MARGIN = 0.3

def embedded(inputs, projection):
    raw_proj = jnp.dot(inputs, projection, preferred_element_type=jnp.float32)
    length = jnp.sqrt(lax.optimization_barrier(jnp.sum(raw_proj * raw_proj, axis=-1, keepdims=True)) + 1e-06)
    return (raw_proj, length)

def permitted(row_index, col_index, language, lang_allow, tile_allow):
    tile_ok = tile_allow[row_index // TILE][:, col_index // TILE] == 1
    pair_ok = lang_allow[language[row_index]][:, language[col_index]] == 1
    return tile_ok & pair_ok | (row_index[:, None] == col_index[None, :])

def scaled_logits(row_block, col_emb, row_index, col_index):
    similar = jnp.dot(row_block, col_emb.T, preferred_element_type=jnp.float32)
    diagonal = (row_index[:, None] == col_index[None, :]).astype(jnp.float32)
    return SCALE * (similar - MARGIN * diagonal)

def backward_proj(inputs, raw_proj, length, upstream, projection):
    unit_vec = raw_proj / length
    dir_grad = ((upstream - unit_vec * lax.optimization_barrier(jnp.sum(unit_vec * upstream, axis=-1, keepdims=True))) / length).astype(jnp.bfloat16)
    grad_in = jnp.dot(dir_grad, projection.T, preferred_element_type=jnp.float32).astype(jnp.bfloat16)
    grad_weight = jnp.dot(inputs.T, dir_grad, preferred_element_type=jnp.float32)
    return (grad_in, grad_weight)

def reference(sources, targets, projection, language, lang_allow, tile_allow):
    src_raw, src_len = embedded(sources, projection)
    tgt_raw, tgt_len = embedded(targets, projection)
    src_unit = (src_raw / src_len).astype(jnp.bfloat16)
    tgt_unit = (tgt_raw / tgt_len).astype(jnp.bfloat16)
    block_rows = math.gcd(PAIRS, 1024)
    count_blocks = PAIRS // block_rows
    blocks = src_unit.reshape(count_blocks, block_rows, D)
    starts = (jnp.arange(count_blocks) * block_rows).astype(jnp.int32)
    col_index = jnp.arange(PAIRS).astype(jnp.int32)

    def first_pass(col_total, element):
        row_block, first_row = element
        row_index = first_row + jnp.arange(block_rows).astype(jnp.int32)
        logits = scaled_logits(row_block, tgt_unit, row_index, col_index)
        allowed = permitted(row_index, col_index, language, lang_allow, tile_allow)
        weights = jnp.where(allowed, jnp.exp(logits - SCALE), jnp.float32(0.0))
        return (col_total + lax.optimization_barrier(jnp.sum(weights, axis=0)), lax.optimization_barrier(jnp.sum(weights, axis=1)))
    col_total, row_total = lax.scan(first_pass, jnp.zeros((PAIRS,), jnp.float32), (blocks, starts))
    row_lse = jnp.log(row_total.reshape(PAIRS)) + SCALE
    col_lse = jnp.log(col_total) + SCALE
    lse_blocks = row_lse.reshape(count_blocks, block_rows)

    def second_pass(tgt_grad, element):
        row_block, first_row, lse_rows = element
        row_index = first_row + jnp.arange(block_rows).astype(jnp.int32)
        logits = scaled_logits(row_block, tgt_unit, row_index, col_index)
        allowed = permitted(row_index, col_index, language, lang_allow, tile_allow)
        soft_rows = jnp.where(allowed, jnp.exp(logits - lse_rows[:, None]), jnp.float32(0.0))
        soft_cols = jnp.where(allowed, jnp.exp(logits - col_lse[None, :]), jnp.float32(0.0))
        diagonal = (row_index[:, None] == col_index[None, :]).astype(jnp.float32)
        logit_grad = (SCALE * (0.5 * (soft_rows + soft_cols) - diagonal)).astype(jnp.bfloat16)
        src_part = jnp.dot(logit_grad, tgt_unit, preferred_element_type=jnp.float32)
        tgt_grad = tgt_grad + lax.dot_general(logit_grad, row_block, (((0,), (0,)), ((), ())), preferred_element_type=jnp.float32)
        return (tgt_grad, src_part)
    tgt_grad, src_parts = lax.scan(second_pass, jnp.zeros((PAIRS, D), jnp.float32), (blocks, starts, lse_blocks))
    src_grad = src_parts.reshape(PAIRS, D)
    grad_sources, weight_src = backward_proj(sources, src_raw, src_len, src_grad, projection)
    grad_targets, weight_tgt = backward_proj(targets, tgt_raw, tgt_len, tgt_grad, projection)
    return (grad_sources, grad_targets, weight_src + weight_tgt)
```

```python
import functools

import jax
import jax.numpy as jnp
from jax import lax
from jax.experimental import pallas as pl
from jax.experimental.pallas import tpu as pltpu
from jax.sharding import PartitionSpec as P

TILE = 512
LANES = 128
SCALE = 20.0
MARGIN = 0.3
YN = 2
BF16 = jnp.bfloat16
F32 = jnp.float32
MESH = pl.DeviceIdType.MESH


def mm(a, b, ca, cb):
    return lax.dot_general(a, b, (((ca,), (cb,)), ((), ())), preferred_element_type=F32)


def fused(
    RN, ZN, PR, PC,
    src_ref, tgt_ref, proj_ref, lang_ref, allow_ref, tile_ref,
    gsrc_ref, gtgt_ref, gproj_ref,
    sraw, traw, sun, tun, lang_cols, mask, e_ref, g_ref,
    rowx, colx, ssend, srecv, tsend, trecv, salong, ralong, talong, qalong,
    w_ref, wsend, wrecv, zsend, zrecv, zfin, wfin, acc,
    zs_sem, zr_sem, qs_sem, qr_sem,
):
    QN = RN * YN
    B, D = src_ref.shape
    cols = QN * B
    row = lax.axis_index("row")
    col = lax.axis_index("col")
    y = lax.rem(col, YN)
    z = col // YN
    q = y * RN + row
    CN = ZN * YN

    def zpeer(d):
        return lax.rem(z + d, ZN)

    def qpeer(d):
        return lax.rem(q + d, QN)

    def zdev(t):
        return (row, t * YN + y)

    def qdev(t):
        return (lax.rem(t, RN), z * YN + t // RN)

    sends = []

    def zsend_one(k, d, src, dst):
        t = zpeer(d)
        c = pltpu.make_async_remote_copy(
            src, dst, zs_sem.at[k, d], zr_sem.at[k, z], device_id=zdev(t), device_id_type=MESH
        )
        c.start()
        sends.append(c)

    def qsend_one(k, d, src, dst):
        t = qpeer(d)
        c = pltpu.make_async_remote_copy(
            src, dst, qs_sem.at[k, d], qr_sem.at[k, q], device_id=qdev(t), device_id_type=MESH
        )
        c.start()
        sends.append(c)

    def zwait(k, d, buf):
        t = zpeer(d)
        pltpu.make_async_remote_copy(
            buf.at[t], buf.at[t], zs_sem.at[k, d], zr_sem.at[k, t],
            device_id=zdev(t), device_id_type=MESH,
        ).wait_recv()
        return t

    def qwait(k, d, buf):
        t = qpeer(d)
        pltpu.make_async_remote_copy(
            buf.at[t], buf.at[t], qs_sem.at[k, d], qr_sem.at[k, t],
            device_id=qdev(t), device_id_type=MESH,
        ).wait_recv()
        return t

    barrier = pltpu.get_barrier_semaphore()
    for d in range(1, ZN):
        pl.semaphore_signal(barrier, inc=1, device_id=zdev(zpeer(d)), device_id_type=MESH)
    for d in range(1, QN):
        pl.semaphore_signal(barrier, inc=1, device_id=qdev(qpeer(d)), device_id_type=MESH)

    def embed(inp, raw):
        r = mm(inp[...], proj_ref[...], 1, 0)
        raw[...] = r
        length = jnp.sqrt(jnp.sum(r * r, axis=-1, keepdims=True) + 1e-06)
        return (r / length).astype(BF16)

    sun[z] = embed(src_ref, sraw)
    tun[q] = embed(tgt_ref, traw)
    pl.semaphore_wait(barrier, ZN + QN - 2)
    for d in range(1, ZN):
        zsend_one(0, d, sun.at[z], sun.at[z])
    for d in range(1, QN):
        qsend_one(0, d, tun.at[q], tun.at[q])

    kind = lax.broadcasted_iota(jnp.int32, (LANES, B), 0)

    def one_hot(block):
        return jnp.where(kind == lang_ref[pl.ds(block, 1), :], 1.0, 0.0).astype(BF16)

    for t in range(QN):
        lang_cols[:, t * B : (t + 1) * B] = mm(
            allow_ref[...], one_hot(z * QN + t), 1, 0
        ).astype(BF16)

    def diagonal(s):
        rows = lax.broadcasted_iota(jnp.int32, (B, cols), 0) + (row * CN + s * YN + y) * B
        colid = lax.broadcasted_iota(jnp.int32, (B, cols), 1) + z * cols
        return rows == colid

    def mask_step(s, c):
        sb = row * CN + s * YN + y
        ok = mm(one_hot(sb), lang_cols[...], 0, 0)
        for t in range(QN):
            allow = tile_ref[sb * B // TILE, (z * QN + t) * B // TILE]
            part = ok[:, t * B : (t + 1) * B]
            mask[s, :, t * B : (t + 1) * B] = jnp.where(allow == 1, part, 0.0)
        return c

    lax.fori_loop(0, ZN, mask_step, 0)

    for d in range(1, ZN):
        zwait(0, d, sun)
    for d in range(1, QN):
        qwait(0, d, tun)

    colx[q] = jnp.zeros((1, cols), F32)

    def totals_step(s, c):
        diag = diagonal(s)
        sim = mm(sun[s], tun[...].reshape(cols, D), 1, 1)
        logits = SCALE * (sim - jnp.where(diag, MARGIN, 0.0))
        e = jnp.where(diag | (mask[s] > 0.5), jnp.exp(logits - SCALE), 0.0)
        e_ref[s] = e
        part = e[:, :LANES]
        for t in range(1, cols // LANES):
            part += e[:, t * LANES : (t + 1) * LANES]
        rowx[z, pl.ds(s, 1), :] = jnp.sum(part.T, axis=0, keepdims=True)
        colx[q] += jnp.sum(e, axis=0, keepdims=True)
        return c

    lax.fori_loop(0, ZN, totals_step, 0)
    for d in range(1, ZN):
        zsend_one(1, d, rowx.at[z], rowx.at[z])
    for d in range(1, QN):
        qsend_one(1, d, colx.at[q], colx.at[q])
    for d in range(1, ZN):
        zwait(1, d, rowx)
    for d in range(1, QN):
        qwait(1, d, colx)
    row_inv = (0.5 * SCALE) / jnp.sum(rowx[...], axis=0)
    rowx_inv = acc
    rowx_inv[0:ZN, 0:B] = row_inv
    col_inv = (0.5 * SCALE) / jnp.sum(colx[...], axis=0)

    def grad_block(s):
        inv = rowx_inv[pl.ds(s, 1), 0:B]
        inv = jnp.broadcast_to(inv, (B, B)).T[:, :1]
        g = e_ref[s] * (inv + col_inv) - jnp.where(diagonal(s), SCALE, 0.0)
        g = g.astype(BF16)
        for t in range(QN):
            g_ref[t, pl.ds(pl.multiple_of(s * B, B), B), :] = g[:, t * B : (t + 1) * B]
        return mm(g, tun[...].reshape(cols, D), 1, 0)

    def split(part, unit):
        u = unit.astype(F32)
        along = jnp.sum(part * u, axis=-1, keepdims=True)
        rest = part - along * u
        return rest.astype(BF16), jnp.broadcast_to(along, (B, B)).T[:1, :]

    for d in range(1, ZN):
        s = zpeer(d)
        rest, along = split(grad_block(s), sun[s])
        ssend[s] = rest
        salong[s] = along
        zsend_one(2, d, ssend.at[s], srecv.at[z])
        zsend_one(5, d, salong.at[s], ralong.at[z])
    src_grad = grad_block(z)
    for d in range(1, QN):
        t = qpeer(d)
        rest, along = split(mm(g_ref[t], sun[...].reshape(ZN * B, D), 0, 0), tun[t])
        tsend[t] = rest
        talong[t] = along
        qsend_one(2, d, tsend.at[t], trecv.at[q])
        qsend_one(5, d, talong.at[t], qalong.at[q])
    tgt_grad = mm(g_ref[q], sun[...].reshape(ZN * B, D), 0, 0)

    def direction(raw, grad):
        r = raw[...]
        length = jnp.sqrt(jnp.sum(r * r, axis=-1, keepdims=True) + 1e-06)
        unit = r / length
        return (
            (grad - unit * jnp.sum(unit * grad, axis=-1, keepdims=True)) / length
        ).astype(BF16)

    def along_unit(along, unit):
        return jnp.broadcast_to(along, (B, B)).T[:, :1] * unit.astype(F32)

    along = jnp.zeros((1, B), F32)
    for d in range(1, QN):
        t = qwait(2, d, trecv)
        qwait(5, d, qalong)
        tgt_grad += trecv[t].astype(F32)
        along += qalong[t]
    tgt_grad += along_unit(along, tun[q])
    tgt_dir = direction(traw, tgt_grad)
    along = jnp.zeros((1, B), F32)
    for d in range(1, ZN):
        s = zwait(2, d, srecv)
        zwait(5, d, ralong)
        src_grad += srecv[s].astype(F32)
        along += ralong[s]
    src_grad += along_unit(along, sun[z])
    src_dir = direction(sraw, src_grad)

    w_ref[...] = mm(
        jnp.concatenate([src_ref[...], tgt_ref[...]], axis=0),
        jnp.concatenate([src_dir, tgt_dir], axis=0),
        0, 0,
    )
    W = D // QN
    for d in range(1, QN):
        t = qpeer(d)
        wsend[t] = w_ref[pl.ds(pl.multiple_of(t * W, 16), W), :].astype(BF16)
        qsend_one(3, d, wsend.at[t], wrecv.at[q])
    gsrc_ref[...] = mm(src_dir, proj_ref[...], 1, 1).astype(BF16)
    gtgt_ref[...] = mm(tgt_dir, proj_ref[...], 1, 1).astype(BF16)
    total = w_ref[pl.ds(pl.multiple_of(q * W, 16), W), :]
    for d in range(1, QN):
        t = qwait(3, d, wrecv)
        total += wrecv[t].astype(F32)
    HR, HC = W // PR, D // PC
    for p in range(ZN):
        a, b = p // PC, p % PC
        zsend[p] = total[a * HR : (a + 1) * HR, b * HC : (b + 1) * HC]
    for d in range(1, ZN):
        s = zpeer(d)
        zsend_one(3, d, zsend.at[s], zrecv.at[z])
    piece = zsend[z]
    for d in range(1, ZN):
        s = zwait(3, d, zrecv)
        piece += zrecv[s]
    zfin[z] = piece.astype(BF16)
    for d in range(1, ZN):
        zsend_one(4, d, zfin.at[z], zfin.at[z])
    for d in range(1, ZN):
        zwait(4, d, zfin)
    for p in range(ZN):
        a, b = p // PC, p % PC
        wfin[q, a * HR : (a + 1) * HR, b * HC : (b + 1) * HC] = zfin[p]
    for d in range(1, QN):
        qsend_one(4, d, wfin.at[q], wfin.at[q])
    gproj_ref[pl.ds(pl.multiple_of(q * W, 16), W), :] = wfin[q].astype(F32)
    for d in range(1, QN):
        t = qwait(4, d, wfin)
        gproj_ref[pl.ds(pl.multiple_of(t * W, 16), W), :] = wfin[t].astype(F32)
    for c in sends:
        c.wait_send()


def fused_device(RN, CN, PR, PC, sources, targets, projection, language, lang_allow, tile_allow):
    ZN, QN = CN // YN, RN * YN
    B, D = sources.shape
    W = D // QN
    pad = LANES - lang_allow.shape[0]
    allow = jnp.pad(lang_allow.astype(BF16), ((0, pad), (0, pad)))
    vmem = pl.BlockSpec(memory_space=pltpu.VMEM)
    smem = pl.BlockSpec(memory_space=pltpu.SMEM)
    V = pltpu.VMEM
    return pl.pallas_call(
        functools.partial(fused, RN, ZN, PR, PC),
        out_shape=(
            jax.ShapeDtypeStruct((B, D), BF16),
            jax.ShapeDtypeStruct((B, D), BF16),
            jax.ShapeDtypeStruct((D, D), F32),
        ),
        in_specs=[vmem] * 5 + [smem],
        out_specs=(vmem,) * 3,
        scratch_shapes=[
            V((B, D), F32),
            V((B, D), F32),
            V((ZN, B, D), BF16),
            V((QN, B, D), BF16),
            V((LANES, QN * B), BF16),
            V((ZN, B, QN * B), F32),
            V((ZN, B, QN * B), F32),
            V((QN, ZN * B, B), BF16),
            V((ZN, ZN, B), F32),
            V((QN, 1, QN * B), F32),
            V((ZN, B, D), BF16),
            V((ZN, B, D), BF16),
            V((QN, B, D), BF16),
            V((QN, B, D), BF16),
            V((ZN, 1, B), F32),
            V((ZN, 1, B), F32),
            V((QN, 1, B), F32),
            V((QN, 1, B), F32),
            V((D, D), F32),
            V((QN, W, D), BF16),
            V((QN, W, D), BF16),
            V((ZN, W // PR, D // PC), F32),
            V((ZN, W // PR, D // PC), F32),
            V((ZN, W // PR, D // PC), BF16),
            V((QN, W, D), BF16),
            V((8, B), F32),
            pltpu.SemaphoreType.DMA((6, ZN)),
            pltpu.SemaphoreType.DMA((6, ZN)),
            pltpu.SemaphoreType.DMA((6, QN)),
            pltpu.SemaphoreType.DMA((6, QN)),
        ],
        compiler_params=pltpu.CompilerParams(
            collective_id=0, has_side_effects=True, vmem_limit_bytes=48 * 2**20
        ),
    )(sources, targets, projection, language.reshape(-1, B), allow, tile_allow)


def embedded(inputs, projection):
    raw_proj = jnp.dot(inputs, projection, preferred_element_type=jnp.float32)
    length = jnp.sqrt(jnp.sum(raw_proj * raw_proj, axis=-1, keepdims=True) + 1e-06)
    return (raw_proj, length)


def permitted(row_index, col_index, language, lang_allow, tile_allow):
    tile_cols = jnp.take(tile_allow, col_index // TILE, axis=1)
    tile_ok = jnp.take(tile_cols, row_index // TILE, axis=0)
    row_lang = lax.dynamic_slice_in_dim(language, row_index[0], row_index.shape[0])
    col_lang = lax.dynamic_slice_in_dim(language, col_index[0], col_index.shape[0])
    lang_cols = jnp.take(lang_allow, col_lang, axis=1)
    pair_ok = jnp.take(lang_cols, row_lang, axis=0)
    return (tile_ok * pair_ok == 1) | (row_index[:, None] == col_index[None, :])


def backward_proj(inputs, raw_proj, length, upstream, projection):
    unit_vec = raw_proj / length
    dir_grad = (
        (upstream - unit_vec * jnp.sum(unit_vec * upstream, axis=-1, keepdims=True)) / length
    ).astype(jnp.bfloat16)
    grad_in = jnp.dot(dir_grad, projection.T, preferred_element_type=jnp.float32).astype(
        jnp.bfloat16
    )
    grad_weight = jnp.dot(inputs.T, dir_grad, preferred_element_type=jnp.float32)
    return (grad_in, grad_weight)


def per_device(sources, targets, projection, language, lang_allow, tile_allow):
    src_raw, src_len = embedded(sources, projection)
    tgt_raw, tgt_len = embedded(targets, projection)
    src_unit = (src_raw / src_len).astype(jnp.bfloat16)
    tgt_unit = (tgt_raw / tgt_len).astype(jnp.bfloat16)
    row_emb = lax.all_gather(src_unit, "col", axis=0, tiled=True)
    col_emb = lax.all_gather(tgt_unit, "row", axis=0, tiled=True)
    row_count = row_emb.shape[0]
    col_count = col_emb.shape[0]
    row_begin = lax.axis_index("row") * row_count
    col_begin = lax.axis_index("col") * col_count
    row_index = row_begin + jnp.arange(row_count)
    col_index = col_begin + jnp.arange(col_count)
    allowed = permitted(row_index, col_index, language, lang_allow, tile_allow)
    similar = jnp.dot(row_emb, col_emb.T, preferred_element_type=jnp.float32)
    diagonal = (row_index[:, None] == col_index[None, :]).astype(jnp.float32)
    logits = SCALE * (similar - MARGIN * diagonal)
    weights = jnp.where(allowed, jnp.exp(logits - SCALE), jnp.float32(0.0))
    row_part = jnp.sum(weights, axis=1)
    col_part = jnp.sum(weights, axis=0)
    row_total = lax.psum(row_part, "col")
    col_total = lax.psum(col_part, "row")
    row_lse = jnp.log(row_total) + SCALE
    col_lse = jnp.log(col_total) + SCALE
    soft_rows = jnp.where(allowed, jnp.exp(logits - row_lse[:, None]), jnp.float32(0.0))
    soft_cols = jnp.where(allowed, jnp.exp(logits - col_lse[None, :]), jnp.float32(0.0))
    logit_grad = (SCALE * (0.5 * (soft_rows + soft_cols) - diagonal)).astype(jnp.bfloat16)
    src_terms = jnp.dot(logit_grad, col_emb, preferred_element_type=jnp.float32)
    src_grad = lax.psum_scatter(src_terms, "col", scatter_dimension=0, tiled=True)
    tgt_terms = lax.dot_general(
        logit_grad, row_emb, (((0,), (0,)), ((), ())), preferred_element_type=jnp.float32
    )
    tgt_grad = lax.psum_scatter(tgt_terms, "row", scatter_dimension=0, tiled=True)
    grad_sources, weight_src = backward_proj(sources, src_raw, src_len, src_grad, projection)
    grad_targets, weight_tgt = backward_proj(targets, tgt_raw, tgt_len, tgt_grad, projection)
    grad_proj = lax.psum(weight_src + weight_tgt, ("row", "col"))
    return (grad_sources, grad_targets, grad_proj)


def pieces(ZN, W, D):
    for PR in (1, 2, 4):
        if ZN % PR == 0 and W % (16 * PR) == 0 and D % (LANES * (ZN // PR)) == 0:
            return PR, ZN // PR
    return None


def solution(mesh):
    RN, CN = mesh.shape["row"], mesh.shape["col"]

    def device(sources, targets, projection, language, lang_allow, tile_allow):
        B, D = sources.shape
        split = None
        if CN % YN == 0 and D % (16 * RN * YN) == 0 and B == LANES and RN * CN <= 64:
            split = pieces(CN // YN, D // (RN * YN), D)
        args = (sources, targets, projection, language, lang_allow, tile_allow)
        if split is None or lang_allow.shape[0] > LANES:
            return per_device(*args)
        return fused_device(RN, CN, *split, *args)

    return jax.shard_map(
        device,
        mesh=mesh,
        in_specs=(P(("row", "col"), None), P(("col", "row"), None), P(), P(), P(), P()),
        out_specs=(P(("row", "col"), None), P(("col", "row"), None), P()),
        check_vma=False,
    )
```

```python
import functools

import jax
import jax.numpy as jnp
from jax import lax
from jax.experimental import pallas as pl
from jax.experimental.pallas import tpu as pltpu
from jax.sharding import PartitionSpec as P

TILE = 512
LANES = 128
SCALE = 20.0
MARGIN = 0.3
YN = 2
CORES = 2
BF16 = jnp.bfloat16
F32 = jnp.float32
MESH = pl.DeviceIdType.MESH


def mm(a, b, ca, cb):
    return lax.dot_general(a, b, (((ca,), (cb,)), ((), ())), preferred_element_type=F32)


def fused(
    RN, ZN, PR, PC,
    src_hbm, tgt_hbm, proj_hbm, lang_hbm, allow_hbm, tile_ref,
    gsrc_hbm, gtgt_hbm, gproj_hbm,
    src_ref, tgt_ref, proj_ref, lang_ref, allow_ref, gsrc_ref, gtgt_ref,
    sraw, traw, sun, tun, lang_cols, mask, e_ref, g_ref,
    rowx, row_inv, colx, ssend, srecv, tcs, tcr, tsend, trecv, salong, ralong, talong, qalong,
    w_ref, wcr, wsend, wrecv, zpart, zsend, zrecv, wfin,
    loc_sem, zs_sem, zr_sem, qs_sem, qr_sem, js_sem, jr_sem, cs_sem, cr_sem,
    fs_sem, fr_sem, hs_sem, hr_sem, out_sem,
):
    QN = RN * YN
    XN = RN // CORES
    JN = XN * YN
    CN = ZN * YN
    B, D = src_ref.shape
    cols = QN * B
    W = D // QN
    HR, HC = W // PR, D // PC
    row = lax.axis_index("row")
    col = lax.axis_index("col")
    y = lax.rem(col, YN)
    z = col // YN
    q = y * RN + row
    core = lax.rem(row, CORES)
    other = 1 - core
    jme = y * XN + row // CORES

    def zpeer(d):
        return lax.rem(z + d, ZN)

    def qpeer(d):
        return lax.rem(q + d, QN)

    def jpeer(d):
        return lax.rem(jme + d, JN)

    def slot(j, c):
        return (j // XN) * RN + lax.rem(j, XN) * CORES + c

    def zdev(t):
        return (row, t * YN + y)

    def qdev(t):
        return (lax.rem(t, RN), z * YN + t // RN)

    def jdev(j):
        return (lax.rem(j, XN) * CORES + core, z * YN + j // XN)

    sibling = (row + 1 - 2 * core, col)

    sends = []

    def push(src, dst, s_sem, r_sem, dev):
        c = pltpu.make_async_remote_copy(src, dst, s_sem, r_sem, device_id=dev, device_id_type=MESH)
        c.start()
        sends.append(c)

    def arrive(buf, s_sem, r_sem, dev):
        pltpu.make_async_remote_copy(
            buf, buf, s_sem, r_sem, device_id=dev, device_id_type=MESH
        ).wait_recv()

    def zpush(k, d, src, dst):
        push(src, dst, zs_sem.at[k, d], zr_sem.at[k, z], zdev(zpeer(d)))

    def zwait(k, d, buf):
        t = zpeer(d)
        arrive(buf, zs_sem.at[k, d], zr_sem.at[k, t], zdev(t))

    def jpush(k, d, src, dst):
        push(src, dst, js_sem.at[k, d], jr_sem.at[k, jme], jdev(jpeer(d)))

    def jwait(k, d, buf):
        j = jpeer(d)
        arrive(buf, js_sem.at[k, d], jr_sem.at[k, j], jdev(j))

    def cpush(k, j, src, dst):
        push(src, dst, cs_sem.at[k, j], cr_sem.at[k, j], sibling)

    def cwait(k, j, buf):
        arrive(buf, cs_sem.at[k, j], cr_sem.at[k, j], sibling)

    barrier = pltpu.get_barrier_semaphore()
    for d in range(1, ZN):
        pl.semaphore_signal(barrier, inc=1, device_id=zdev(zpeer(d)), device_id_type=MESH)
    for d in range(1, QN):
        pl.semaphore_signal(barrier, inc=1, device_id=qdev(qpeer(d)), device_id_type=MESH)
    loads = [
        pltpu.make_async_copy(a, b, loc_sem.at[k])
        for k, (a, b) in enumerate(
            [
                (src_hbm, src_ref), (proj_hbm, proj_ref), (tgt_hbm, tgt_ref),
                (lang_hbm, lang_ref), (allow_hbm, allow_ref),
            ]
        )
    ]
    for c in loads:
        c.start()

    stores = []

    def store(src, dst, sem):
        c = pltpu.make_async_copy(src, dst, sem)
        c.start()
        stores.append(c)

    def embed(inp, raw):
        r = mm(inp[...], proj_ref[...], 1, 0)
        raw[...] = r
        length = jnp.sqrt(jnp.sum(r * r, axis=-1, keepdims=True) + 1e-06)
        return (r / length).astype(BF16)

    loads[0].wait()
    loads[1].wait()
    sun[z] = embed(src_ref, sraw)
    pl.semaphore_wait(barrier, ZN + QN - 2)
    for d in range(1, ZN):
        zpush(0, d, sun.at[z], sun.at[z])
    loads[2].wait()
    tun[q] = embed(tgt_ref, traw)
    for d in range(1, JN):
        jpush(0, d, tun.at[q], tun.at[q])
    cpush(0, jme, tun.at[q], tun.at[q])

    loads[3].wait()
    loads[4].wait()
    NL = allow_ref.shape[0]
    kind = lax.broadcasted_iota(jnp.int32, (NL, B), 0)
    allow = allow_ref[...].astype(F32).astype(BF16)

    def one_hot(block):
        return jnp.where(kind == lang_ref[pl.ds(block, 1), :], 1.0, 0.0).astype(BF16)

    for t in range(QN):
        lang_cols[:, t * B : (t + 1) * B] = mm(allow, one_hot(z * QN + t), 1, 0).astype(BF16)

    def diagonal(s):
        rows = lax.broadcasted_iota(jnp.int32, (B, cols), 0) + (row * CN + s * YN + y) * B
        colid = lax.broadcasted_iota(jnp.int32, (B, cols), 1) + z * cols
        return rows == colid

    def mask_step(s, c):
        sb = row * CN + s * YN + y
        ok = mm(one_hot(sb), lang_cols[...], 0, 0)
        for t in range(QN):
            tile_ok = tile_ref[sb * B // TILE, (z * QN + t) * B // TILE]
            part = ok[:, t * B : (t + 1) * B]
            mask[s, :, t * B : (t + 1) * B] = jnp.where(tile_ok == 1, part, 0.0)
        return c

    lax.fori_loop(0, ZN, mask_step, 0)

    for d in range(1, JN):
        j = jpeer(d)
        t = slot(j, core)
        jwait(0, d, tun.at[t])
        cpush(0, j, tun.at[t], tun.at[t])
    for d in range(JN):
        j = jpeer(d)
        cwait(0, j, tun.at[slot(j, other)])

    colx[q] = jnp.zeros((1, cols), F32)

    def totals(s):
        diag = diagonal(s)
        sim = mm(sun[s], tun[...].reshape(cols, D), 1, 1)
        logits = SCALE * (sim - jnp.where(diag, MARGIN, 0.0))
        e = jnp.where(diag | (mask[s] > 0.5), jnp.exp(logits - SCALE), 0.0)
        e_ref[s] = e
        part = e[:, :LANES]
        for t in range(1, cols // LANES):
            part += e[:, t * LANES : (t + 1) * LANES]
        rowx[z, pl.ds(s, 1), :] = jnp.sum(part.T, axis=0, keepdims=True)
        colx[q] += jnp.sum(e, axis=0, keepdims=True)

    for d in range(ZN):
        s = zpeer(d)
        if d:
            zwait(0, d, sun.at[s])
        totals(s)
    for d in range(1, ZN):
        zpush(1, d, rowx.at[z], rowx.at[z])
    for d in range(1, QN):
        push(colx.at[q], colx.at[q], qs_sem.at[d], qr_sem.at[q], qdev(qpeer(d)))
    for d in range(1, ZN):
        zwait(1, d, rowx.at[zpeer(d)])
    for d in range(1, QN):
        t = qpeer(d)
        arrive(colx.at[t], qs_sem.at[d], qr_sem.at[t], qdev(t))
    row_inv[...] = (0.5 * SCALE) / jnp.sum(rowx[...], axis=0)
    col_inv = (0.5 * SCALE) / jnp.sum(colx[...], axis=0)

    def grad_block(s):
        inv = jnp.broadcast_to(row_inv[pl.ds(s, 1), :], (B, B)).T[:, :1]
        g = e_ref[s] * (inv + col_inv) - jnp.where(diagonal(s), SCALE, 0.0)
        g = g.astype(BF16)
        for t in range(QN):
            g_ref[t, pl.ds(pl.multiple_of(s * B, B), B), :] = g[:, t * B : (t + 1) * B]
        return mm(g, tun[...].reshape(cols, D), 1, 0)

    def split(part, unit):
        u = unit.astype(F32)
        along = jnp.sum(part * u, axis=-1, keepdims=True)
        rest = part - along * u
        return rest.astype(BF16), jnp.broadcast_to(along, (B, B)).T[:1, :]

    def along_unit(along, unit):
        return jnp.broadcast_to(along, (B, B)).T[:, :1] * unit.astype(F32)

    for d in range(1, ZN):
        s = zpeer(d)
        rest, along = split(grad_block(s), sun[s])
        ssend[s] = rest
        salong[s] = along
        zpush(2, d, ssend.at[s], srecv.at[z])
        zpush(5, d, salong.at[s], ralong.at[z])
    src_grad = grad_block(z)

    def tgt_part(t):
        return mm(g_ref[t], sun[...].reshape(ZN * B, D), 0, 0)

    for d in range(1, JN + 1):
        j = jpeer(d)
        tcs[j] = tgt_part(slot(j, other))
        cpush(1, j, tcs.at[j], tcr.at[j])
    for d in range(1, JN):
        j = jpeer(d)
        t = slot(j, core)
        part = tgt_part(t)
        cwait(1, j, tcr.at[j])
        rest, along = split(part + tcr[j], tun[t])
        tsend[j] = rest
        talong[j] = along
        jpush(1, d, tsend.at[j], trecv.at[jme])
        jpush(2, d, talong.at[j], qalong.at[jme])
    tgt_grad = tgt_part(q)
    cwait(1, jme, tcr.at[jme])
    tgt_grad += tcr[jme]

    def direction(raw, grad):
        r = raw[...]
        length = jnp.sqrt(jnp.sum(r * r, axis=-1, keepdims=True) + 1e-06)
        unit = r / length
        return (
            (grad - unit * jnp.sum(unit * grad, axis=-1, keepdims=True)) / length
        ).astype(BF16)

    along = jnp.zeros((1, B), F32)
    for d in range(1, JN):
        j = jpeer(d)
        jwait(1, d, trecv.at[j])
        jwait(2, d, qalong.at[j])
        tgt_grad += trecv[j].astype(F32)
        along += qalong[j]
    tgt_grad += along_unit(along, tun[q])
    tgt_dir = direction(traw, tgt_grad)
    w_ref[...] = mm(tgt_ref[...], tgt_dir, 0, 0)
    gtgt_ref[...] = mm(tgt_dir, proj_ref[...], 1, 1).astype(BF16)
    store(gtgt_ref, gtgt_hbm, loc_sem.at[5])

    along = jnp.zeros((1, B), F32)
    for d in range(1, ZN):
        s = zpeer(d)
        zwait(2, d, srecv.at[s])
        zwait(5, d, ralong.at[s])
        src_grad += srecv[s].astype(F32)
        along += ralong[s]
    src_grad += along_unit(along, sun[z])
    src_dir = direction(sraw, src_grad)

    w_ref[...] += mm(src_ref[...], src_dir, 0, 0)

    def rows_of(t):
        return pl.ds(pl.multiple_of(t * W, 16), W)

    for d in range(1, JN + 1):
        j = jpeer(d)
        cpush(2, j, w_ref.at[rows_of(slot(j, other))], wcr.at[j])
    gsrc_ref[...] = mm(src_dir, proj_ref[...], 1, 1).astype(BF16)
    store(gsrc_ref, gsrc_hbm, loc_sem.at[6])
    for d in range(1, JN):
        j = jpeer(d)
        cwait(2, j, wcr.at[j])
        wsend[j] = (w_ref[rows_of(slot(j, core)), :] + wcr[j]).astype(BF16)
        jpush(3, d, wsend.at[j], wrecv.at[jme])
    cwait(2, jme, wcr.at[jme])
    total = w_ref[rows_of(q), :] + wcr[jme]
    for d in range(1, JN):
        j = jpeer(d)
        jwait(3, d, wrecv.at[j])
        total += wrecv[j].astype(F32)
    for p in range(ZN):
        a, b = p // PC, p % PC
        zpart[p] = total[a * HR : (a + 1) * HR, b * HC : (b + 1) * HC]
    for d in range(1, ZN):
        s = zpeer(d)
        zsend[s] = zpart[s].astype(BF16)
        zpush(3, d, zsend.at[s], zrecv.at[z])
    piece = zpart[z]
    for d in range(1, ZN):
        s = zpeer(d)
        zwait(3, d, zrecv.at[s])
        piece += zrecv[s].astype(F32)
    wfin[q, z] = piece.astype(BF16)
    for d in range(1, ZN):
        zpush(4, d, wfin.at[q, z], wfin.at[q, z])

    def put(t, p):
        r = pl.ds(pl.multiple_of(t * W + (p // PC) * HR, 16), HR)
        c = pl.ds(pl.multiple_of(lax.rem(p, PC) * HC, LANES), HC)
        store(wfin.at[t, p], gproj_hbm.at[r, c], out_sem.at[t, p])

    for k in range(ZN):
        p = zpeer(k)
        if k:
            zwait(4, k, wfin.at[q, p])
        here = wfin.at[q, p]
        for d in range(1, JN):
            push(here, here, fs_sem.at[d, p], fr_sem.at[jme, p], jdev(jpeer(d)))
        push(here, here, hs_sem.at[jme, p], hr_sem.at[jme, p], sibling)
        put(q, p)
    for k in range(ZN):
        p = zpeer(k)
        for d in range(1, JN):
            j = jpeer(d)
            t = slot(j, core)
            here = wfin.at[t, p]
            arrive(here, fs_sem.at[d, p], fr_sem.at[j, p], jdev(j))
            push(here, here, hs_sem.at[j, p], hr_sem.at[j, p], sibling)
            put(t, p)
    for k in range(ZN):
        p = zpeer(k)
        for d in range(JN):
            j = jpeer(d)
            t = slot(j, other)
            arrive(wfin.at[t, p], hs_sem.at[j, p], hr_sem.at[j, p], sibling)
            put(t, p)
    for c in sends:
        c.wait_send()
    for c in stores:
        c.wait()


def fused_device(RN, CN, PR, PC, sources, targets, projection, language, lang_allow, tile_allow):
    ZN, QN, JN = CN // YN, RN * YN, RN * YN // CORES
    B, D = sources.shape
    NL = lang_allow.shape[0]
    W = D // QN
    langs = language.reshape(-1, B)
    smem = pl.BlockSpec(memory_space=pltpu.SMEM)
    hbm = pl.BlockSpec(memory_space=pltpu.HBM)
    V = pltpu.VMEM
    S = pltpu.SemaphoreType.DMA
    piece = (ZN, W // PR, D // PC)
    grad_sources, grad_targets, grad_proj = pl.pallas_call(
        functools.partial(fused, RN, ZN, PR, PC),
        out_shape=(
            jax.ShapeDtypeStruct((B, D), BF16),
            jax.ShapeDtypeStruct((B, D), BF16),
            jax.ShapeDtypeStruct((D, D), BF16),
        ),
        in_specs=[hbm] * 5 + [smem],
        out_specs=(hbm,) * 3,
        scratch_shapes=[
            V((B, D), BF16),
            V((B, D), BF16),
            V((D, D), BF16),
            V(langs.shape, jnp.int32),
            V((NL, NL), jnp.int32),
            V((B, D), BF16),
            V((B, D), BF16),
            V((B, D), F32),
            V((B, D), F32),
            V((ZN, B, D), BF16),
            V((QN, B, D), BF16),
            V((NL, QN * B), BF16),
            V((ZN, B, QN * B), F32),
            V((ZN, B, QN * B), F32),
            V((QN, ZN * B, B), BF16),
            V((ZN, ZN, B), F32),
            V((ZN, B), F32),
            V((QN, 1, QN * B), F32),
            V((ZN, B, D), BF16),
            V((ZN, B, D), BF16),
            V((JN, B, D), F32),
            V((JN, B, D), F32),
            V((JN, B, D), BF16),
            V((JN, B, D), BF16),
            V((ZN, 1, B), F32),
            V((ZN, 1, B), F32),
            V((JN, 1, B), F32),
            V((JN, 1, B), F32),
            V((D, D), F32),
            V((JN, W, D), F32),
            V((JN, W, D), BF16),
            V((JN, W, D), BF16),
            V(piece, F32),
            V(piece, BF16),
            V(piece, BF16),
            V((QN, *piece), BF16),
            S((7,)),
            S((6, ZN)),
            S((6, ZN)),
            S((QN,)),
            S((QN,)),
            S((4, JN)),
            S((4, JN)),
            S((3, JN)),
            S((3, JN)),
            S((JN, ZN)),
            S((JN, ZN)),
            S((JN, ZN)),
            S((JN, ZN)),
            S((QN, ZN)),
        ],
        compiler_params=pltpu.CompilerParams(
            collective_id=0, has_side_effects=True, vmem_limit_bytes=60 * 2**20
        ),
    )(sources, targets, projection, langs, lang_allow, tile_allow)
    return grad_sources, grad_targets, grad_proj.astype(F32)


def embedded(inputs, projection):
    raw_proj = jnp.dot(inputs, projection, preferred_element_type=jnp.float32)
    length = jnp.sqrt(jnp.sum(raw_proj * raw_proj, axis=-1, keepdims=True) + 1e-06)
    return (raw_proj, length)


def permitted(row_index, col_index, language, lang_allow, tile_allow):
    tile_cols = jnp.take(tile_allow, col_index // TILE, axis=1)
    tile_ok = jnp.take(tile_cols, row_index // TILE, axis=0)
    row_lang = lax.dynamic_slice_in_dim(language, row_index[0], row_index.shape[0])
    col_lang = lax.dynamic_slice_in_dim(language, col_index[0], col_index.shape[0])
    lang_cols = jnp.take(lang_allow, col_lang, axis=1)
    pair_ok = jnp.take(lang_cols, row_lang, axis=0)
    return (tile_ok * pair_ok == 1) | (row_index[:, None] == col_index[None, :])


def backward_proj(inputs, raw_proj, length, upstream, projection):
    unit_vec = raw_proj / length
    dir_grad = (
        (upstream - unit_vec * jnp.sum(unit_vec * upstream, axis=-1, keepdims=True)) / length
    ).astype(jnp.bfloat16)
    grad_in = jnp.dot(dir_grad, projection.T, preferred_element_type=jnp.float32).astype(
        jnp.bfloat16
    )
    grad_weight = jnp.dot(inputs.T, dir_grad, preferred_element_type=jnp.float32)
    return (grad_in, grad_weight)


def per_device(sources, targets, projection, language, lang_allow, tile_allow):
    src_raw, src_len = embedded(sources, projection)
    tgt_raw, tgt_len = embedded(targets, projection)
    src_unit = (src_raw / src_len).astype(jnp.bfloat16)
    tgt_unit = (tgt_raw / tgt_len).astype(jnp.bfloat16)
    row_emb = lax.all_gather(src_unit, "col", axis=0, tiled=True)
    col_emb = lax.all_gather(tgt_unit, "row", axis=0, tiled=True)
    row_count = row_emb.shape[0]
    col_count = col_emb.shape[0]
    row_begin = lax.axis_index("row") * row_count
    col_begin = lax.axis_index("col") * col_count
    row_index = row_begin + jnp.arange(row_count)
    col_index = col_begin + jnp.arange(col_count)
    allowed = permitted(row_index, col_index, language, lang_allow, tile_allow)
    similar = jnp.dot(row_emb, col_emb.T, preferred_element_type=jnp.float32)
    diagonal = (row_index[:, None] == col_index[None, :]).astype(jnp.float32)
    logits = SCALE * (similar - MARGIN * diagonal)
    weights = jnp.where(allowed, jnp.exp(logits - SCALE), jnp.float32(0.0))
    row_part = jnp.sum(weights, axis=1)
    col_part = jnp.sum(weights, axis=0)
    row_total = lax.psum(row_part, "col")
    col_total = lax.psum(col_part, "row")
    row_lse = jnp.log(row_total) + SCALE
    col_lse = jnp.log(col_total) + SCALE
    soft_rows = jnp.where(allowed, jnp.exp(logits - row_lse[:, None]), jnp.float32(0.0))
    soft_cols = jnp.where(allowed, jnp.exp(logits - col_lse[None, :]), jnp.float32(0.0))
    logit_grad = (SCALE * (0.5 * (soft_rows + soft_cols) - diagonal)).astype(jnp.bfloat16)
    src_terms = jnp.dot(logit_grad, col_emb, preferred_element_type=jnp.float32)
    src_grad = lax.psum_scatter(src_terms, "col", scatter_dimension=0, tiled=True)
    tgt_terms = lax.dot_general(
        logit_grad, row_emb, (((0,), (0,)), ((), ())), preferred_element_type=jnp.float32
    )
    tgt_grad = lax.psum_scatter(tgt_terms, "row", scatter_dimension=0, tiled=True)
    grad_sources, weight_src = backward_proj(sources, src_raw, src_len, src_grad, projection)
    grad_targets, weight_tgt = backward_proj(targets, tgt_raw, tgt_len, tgt_grad, projection)
    grad_proj = lax.psum(weight_src + weight_tgt, ("row", "col"))
    return (grad_sources, grad_targets, grad_proj)


def pieces(ZN, W, D):
    for PR in (1, 2, 4):
        if ZN % PR == 0 and W % (16 * PR) == 0 and D % (LANES * (ZN // PR)) == 0:
            return PR, ZN // PR
    return None


def solution(mesh):
    RN, CN = mesh.shape["row"], mesh.shape["col"]

    def device(sources, targets, projection, language, lang_allow, tile_allow):
        B, D = sources.shape
        split = None
        if CN % YN == 0 and RN % CORES == 0 and D % (16 * RN * YN) == 0 and B == LANES and RN * CN <= 64:
            split = pieces(CN // YN, D // (RN * YN), D)
        args = (sources, targets, projection, language, lang_allow, tile_allow)
        if split is None:
            return per_device(*args)
        return fused_device(RN, CN, *split, *args)

    return jax.shard_map(
        device,
        mesh=mesh,
        in_specs=(P(("row", "col"), None), P(("col", "row"), None), P(), P(), P(), P()),
        out_specs=(P(("row", "col"), None), P(("col", "row"), None), P()),
        check_vma=False,
    )
```

```python
import functools

import jax
import jax.numpy as jnp
from jax import lax
from jax.experimental import pallas as pl
from jax.experimental.pallas import tpu as pltpu
from jax.sharding import PartitionSpec as P

TILE = 512
LANES = 128
SCALE = 20.0
MARGIN = 0.3
YN = 2
CORES = 2
PARTS = 4
BF16 = jnp.bfloat16
F32 = jnp.float32
MESH = pl.DeviceIdType.MESH


def mm(a, b, ca, cb):
    return lax.dot_general(a, b, (((ca,), (cb,)), ((), ())), preferred_element_type=F32)


def fused(
    RN, ZN, PR, PC,
    src_hbm, tgt_hbm, proj_hbm, lang_hbm, allow_hbm, tile_ref,
    gsrc_hbm, gtgt_hbm, gproj_hbm,
    src_ref, tgt_ref, proj_ref, lang_ref, allow_ref, gsrc_ref, gtgt_ref,
    sraw, traw, sun, tun, lang_cols, mask, e_ref, g_ref,
    rowx, row_inv, colx, ssend, srecv, tcs, tcr, tsend, trecv, salong, ralong, talong, qalong,
    w_ref, wcr, wsend, wrecv, zpart, zsend, zrecv, wfin,
    loc_sem, zs_sem, zr_sem, qs_sem, qr_sem, js_sem, jr_sem, cs_sem, cr_sem,
    fs_sem, fr_sem, hs_sem, hr_sem, out_sem,
    hold, hold_along, passed, passed_along, src_acc, along_acc, rs_sem, rr_sem,
):
    QN = RN * YN
    XN = RN // CORES
    JN = XN * YN
    CN = ZN * YN
    B, D = src_ref.shape
    cols = QN * B
    W = D // QN
    HR, HC = W // PR, D // PC
    row = lax.axis_index("row")
    col = lax.axis_index("col")
    y = lax.rem(col, YN)
    z = col // YN
    q = y * RN + row
    core = lax.rem(row, CORES)
    other = 1 - core
    jme = y * XN + row // CORES

    def zpeer(d):
        return lax.rem(z + d, ZN)

    def qpeer(d):
        return lax.rem(q + d, QN)

    def jpeer(d):
        return lax.rem(jme + d, JN)

    def slot(j, c):
        return (j // XN) * RN + lax.rem(j, XN) * CORES + c

    def zdev(t):
        return (row, t * YN + y)

    def qdev(t):
        return (lax.rem(t, RN), z * YN + t // RN)

    def jdev(j):
        return (lax.rem(j, XN) * CORES + core, z * YN + j // XN)

    sibling = (row + 1 - 2 * core, col)

    sends = []

    def push(src, dst, s_sem, r_sem, dev, cond=None):
        c = pltpu.make_async_remote_copy(src, dst, s_sem, r_sem, device_id=dev, device_id_type=MESH)
        if cond is None:
            c.start()
        else:
            pl.when(cond)(c.start)
        sends.append((c, cond))

    def arrive(buf, s_sem, r_sem, dev):
        pltpu.make_async_remote_copy(
            buf, buf, s_sem, r_sem, device_id=dev, device_id_type=MESH
        ).wait_recv()

    last = ZN - 1
    relays = ZN == 4

    def far(t):
        return ((z == 0) & (t == last)) | ((z == last) & (t == 0))

    def middle(t):
        return ((z == last - 1) & (t == 0)) | ((z == 1) & (t == last))

    def no(c):
        return jnp.logical_not(c)

    near_first = sorted(range(1, ZN), key=lambda d: abs(2 * d - ZN))
    far_first = near_first[::-1]

    def zpush(k, d, src, dst, cond=None):
        push(src, dst, zs_sem.at[k, d], zr_sem.at[k, z], zdev(zpeer(d)), cond)

    def zwait(k, d, buf):
        t = zpeer(d)
        arrive(buf, zs_sem.at[k, d], zr_sem.at[k, t], zdev(t))

    def jpush(k, d, src, dst):
        push(src, dst, js_sem.at[k, d], jr_sem.at[k, jme], jdev(jpeer(d)))

    def jwait(k, d, buf):
        j = jpeer(d)
        arrive(buf, js_sem.at[k, d], jr_sem.at[k, j], jdev(j))

    def cpush(k, j, src, dst):
        push(src, dst, cs_sem.at[k, j], cr_sem.at[k, j], sibling)

    def cwait(k, j, buf):
        arrive(buf, cs_sem.at[k, j], cr_sem.at[k, j], sibling)

    barrier = pltpu.get_barrier_semaphore()
    for d in range(1, ZN):
        pl.semaphore_signal(barrier, inc=1, device_id=zdev(zpeer(d)), device_id_type=MESH)
    for d in range(1, QN):
        pl.semaphore_signal(barrier, inc=1, device_id=qdev(qpeer(d)), device_id_type=MESH)
    loads = [
        pltpu.make_async_copy(a, b, loc_sem.at[k])
        for k, (a, b) in enumerate(
            [
                (src_hbm, src_ref), (proj_hbm, proj_ref), (tgt_hbm, tgt_ref),
                (lang_hbm, lang_ref), (allow_hbm, allow_ref),
            ]
        )
    ]
    for c in loads:
        c.start()

    stores = []

    def store(src, dst, sem):
        c = pltpu.make_async_copy(src, dst, sem)
        c.start()
        stores.append(c)

    def embed(inp, raw):
        r = mm(inp[...], proj_ref[...], 1, 0)
        raw[...] = r
        length = jnp.sqrt(jnp.sum(r * r, axis=-1, keepdims=True) + 1e-06)
        return (r / length).astype(BF16)

    loads[0].wait()
    loads[1].wait()
    sun[z] = embed(src_ref, sraw)
    pl.semaphore_wait(barrier, ZN + QN - 2)
    for d in near_first:
        zpush(0, d, sun.at[z], sun.at[z], no(far(zpeer(d))) if relays else None)
    loads[2].wait()
    tun[q] = embed(tgt_ref, traw)
    for d in range(1, JN):
        jpush(0, d, tun.at[q], tun.at[q])
    cpush(0, jme, tun.at[q], tun.at[q])

    loads[3].wait()
    loads[4].wait()
    NL = allow_ref.shape[0]
    kind = lax.broadcasted_iota(jnp.int32, (NL, B), 0)
    allow = allow_ref[...].astype(F32).astype(BF16)

    def one_hot(block):
        return jnp.where(kind == lang_ref[pl.ds(block, 1), :], 1.0, 0.0).astype(BF16)

    for t in range(QN):
        lang_cols[:, t * B : (t + 1) * B] = mm(allow, one_hot(z * QN + t), 1, 0).astype(BF16)

    def diagonal(s):
        rows = lax.broadcasted_iota(jnp.int32, (B, cols), 0) + (row * CN + s * YN + y) * B
        colid = lax.broadcasted_iota(jnp.int32, (B, cols), 1) + z * cols
        return rows == colid

    def mask_step(s, c):
        sb = row * CN + s * YN + y
        ok = mm(one_hot(sb), lang_cols[...], 0, 0)
        for t in range(QN):
            tile_ok = tile_ref[sb * B // TILE, (z * QN + t) * B // TILE]
            part = ok[:, t * B : (t + 1) * B]
            mask[s, :, t * B : (t + 1) * B] = jnp.where(tile_ok == 1, part, 0.0)
        return c

    lax.fori_loop(0, ZN, mask_step, 0)

    for d in range(1, JN):
        j = jpeer(d)
        t = slot(j, core)
        jwait(0, d, tun.at[t])
        cpush(0, j, tun.at[t], tun.at[t])
    for d in range(JN):
        j = jpeer(d)
        cwait(0, j, tun.at[slot(j, other)])

    colx[q] = jnp.zeros((1, cols), F32)

    def totals(s):
        diag = diagonal(s)
        sim = mm(sun[s], tun[...].reshape(cols, D), 1, 1)
        logits = SCALE * (sim - jnp.where(diag, MARGIN, 0.0))
        e = jnp.where(diag | (mask[s] > 0.5), jnp.exp(logits - SCALE), 0.0)
        e_ref[s] = e
        part = e[:, :LANES]
        for t in range(1, cols // LANES):
            part += e[:, t * LANES : (t + 1) * LANES]
        rowx[z, pl.ds(s, 1), :] = jnp.sum(part.T, axis=0, keepdims=True)
        colx[q] += jnp.sum(e, axis=0, keepdims=True)

    totals(z)
    if relays:
        d = near_first[0]
        s = zpeer(d)
        pl.when(middle(s))(functools.partial(zwait, 0, d, sun.at[s]))
        push(sun.at[s], sun.at[s], rs_sem.at[2], zr_sem.at[0, s], zdev(last - s), middle(s))
        first = 1 + lax.rem(z, 2)
        final = last * (1 - z // 2)
        order = [first, last * 2 - z - first - final, final]
    else:
        order = [zpeer(d) for d in range(1, ZN)]

    def take(s):
        arrive(sun.at[s], zs_sem.at[0, 1], zr_sem.at[0, s], zdev(s))

    for k, s in enumerate(order):
        if relays and k == len(order) - 1:
            pl.when(no(middle(s)))(functools.partial(take, s))
        else:
            take(s)
        totals(s)
    for d in range(1, ZN):
        zpush(1, d, rowx.at[z], rowx.at[z])
    for d in range(1, QN):
        push(colx.at[q], colx.at[q], qs_sem.at[d], qr_sem.at[q], qdev(qpeer(d)))
    for d in range(1, ZN):
        zwait(1, d, rowx.at[zpeer(d)])
    for d in range(1, QN):
        t = qpeer(d)
        arrive(colx.at[t], qs_sem.at[d], qr_sem.at[t], qdev(t))
    row_inv[...] = (0.5 * SCALE) / jnp.sum(rowx[...], axis=0)
    col_inv = (0.5 * SCALE) / jnp.sum(colx[...], axis=0)

    def grad_block(s):
        inv = jnp.broadcast_to(row_inv[pl.ds(s, 1), :], (B, B)).T[:, :1]
        g = e_ref[s] * (inv + col_inv) - jnp.where(diagonal(s), SCALE, 0.0)
        g = g.astype(BF16)
        for t in range(QN):
            g_ref[t, pl.ds(pl.multiple_of(s * B, B), B), :] = g[:, t * B : (t + 1) * B]
        return mm(g, tun[...].reshape(cols, D), 1, 0)

    def split(part, unit):
        u = unit.astype(F32)
        along = jnp.sum(part * u, axis=-1, keepdims=True)
        rest = part - along * u
        return rest.astype(BF16), jnp.broadcast_to(along, (B, B)).T[:1, :]

    def along_unit(along, unit):
        return jnp.broadcast_to(along, (B, B)).T[:, :1] * unit.astype(F32)

    def send_sources(d, cond=None):
        s = zpeer(d)
        zpush(2, d, ssend.at[s], srecv.at[z], cond)
        zpush(5, d, salong.at[s], ralong.at[z], cond)

    for d in far_first:
        s = zpeer(d)
        part = grad_block(s)
        u = sun[s].astype(F32)
        along = jnp.sum(part * u, axis=-1, keepdims=True)
        rest = part - along * u
        along = jnp.broadcast_to(along, (B, B)).T[:1, :]
        ssend[s] = rest.astype(BF16)
        salong[s] = along
        if not relays:
            send_sources(d)
        elif d == near_first[0]:
            hold[...] = rest
            hold_along[...] = along
            send_sources(d, no(middle(s)))
        else:
            send_sources(d, no(far(s)))
            by = z + 1 - 2 * lax.rem(z, 2)
            if d in (1, last):
                k = 0 if d == 1 else 3
                push(ssend.at[s], passed, rs_sem.at[k], rr_sem.at[0], zdev(by), far(s))
                push(salong.at[s], passed_along, rs_sem.at[k + 1], rr_sem.at[1], zdev(by), far(s))
    src_grad = grad_block(z)

    def tgt_part(t):
        return mm(g_ref[t], sun[...].reshape(ZN * B, D), 0, 0)

    for d in range(1, JN + 1):
        j = jpeer(d)
        tcs[j] = tgt_part(slot(j, other))
        cpush(1, j, tcs.at[j], tcr.at[j])
    if relays:
        d = near_first[0]
        s = zpeer(d)

        @pl.when(middle(s))
        def _():
            end = zdev(last - s)
            arrive(passed, rs_sem.at[0], rr_sem.at[0], end)
            arrive(passed_along, rs_sem.at[1], rr_sem.at[1], end)
            ssend[s] = (hold[...] + passed[...].astype(F32)).astype(BF16)
            salong[s] = hold_along[...] + passed_along[...]

        send_sources(d, middle(s))
    for d in range(1, JN):
        j = jpeer(d)
        t = slot(j, core)
        part = tgt_part(t)
        cwait(1, j, tcr.at[j])
        rest, along = split(part + tcr[j], tun[t])
        tsend[j] = rest
        talong[j] = along
        jpush(1, d, tsend.at[j], trecv.at[jme])
        jpush(2, d, talong.at[j], qalong.at[jme])
    tgt_grad = tgt_part(q)
    cwait(1, jme, tcr.at[jme])
    tgt_grad += tcr[jme]

    def direction(raw, grad):
        r = raw[...]
        length = jnp.sqrt(jnp.sum(r * r, axis=-1, keepdims=True) + 1e-06)
        unit = r / length
        return (
            (grad - unit * jnp.sum(unit * grad, axis=-1, keepdims=True)) / length
        ).astype(BF16)

    along = jnp.zeros((1, B), F32)
    for d in range(1, JN):
        j = jpeer(d)
        jwait(1, d, trecv.at[j])
        jwait(2, d, qalong.at[j])
        tgt_grad += trecv[j].astype(F32)
        along += qalong[j]
    tgt_grad += along_unit(along, tun[q])
    tgt_dir = direction(traw, tgt_grad)
    w_ref[...] = mm(tgt_ref[...], tgt_dir, 0, 0)
    gtgt_ref[...] = mm(tgt_dir, proj_ref[...], 1, 1).astype(BF16)
    store(gtgt_ref, gtgt_hbm, loc_sem.at[5])

    src_acc[...] = src_grad
    along_acc[...] = jnp.zeros((1, B), F32)
    for d in range(1, ZN):
        s = zpeer(d)

        def add(d=d, s=s):
            zwait(2, d, srecv.at[s])
            zwait(5, d, ralong.at[s])
            src_acc[...] += srecv[s].astype(F32)
            along_acc[...] += ralong[s]

        if relays:
            pl.when(no(far(s)))(add)
        else:
            add()
    src_grad = src_acc[...] + along_unit(along_acc[...], sun[z])
    src_dir = direction(sraw, src_grad)

    w_ref[...] += mm(src_ref[...], src_dir, 0, 0)

    def rows_of(t):
        return pl.ds(pl.multiple_of(t * W, 16), W)

    for d in range(1, JN + 1):
        j = jpeer(d)
        cpush(2, j, w_ref.at[rows_of(slot(j, other))], wcr.at[j])
    gsrc_ref[...] = mm(src_dir, proj_ref[...], 1, 1).astype(BF16)
    store(gsrc_ref, gsrc_hbm, loc_sem.at[6])
    for d in range(1, JN):
        j = jpeer(d)
        cwait(2, j, wcr.at[j])
        wsend[j] = (w_ref[rows_of(slot(j, core)), :] + wcr[j]).astype(BF16)
        jpush(3, d, wsend.at[j], wrecv.at[jme])
    cwait(2, jme, wcr.at[jme])
    total = w_ref[rows_of(q), :] + wcr[jme]
    for d in range(1, JN):
        j = jpeer(d)
        jwait(3, d, wrecv.at[j])
        total += wrecv[j].astype(F32)
    for p in range(ZN):
        a, b = p // PC, p % PC
        zpart[p] = total[a * HR : (a + 1) * HR, b * HC : (b + 1) * HC]
    for d in range(1, ZN):
        s = zpeer(d)
        zsend[s] = zpart[s].astype(BF16)
        zpush(3, d, zsend.at[s], zrecv.at[z])
    piece = zpart[z]
    for d in range(1, ZN):
        s = zpeer(d)
        zwait(3, d, zrecv.at[s])
        piece += zrecv[s].astype(F32)
    wfin[q, z] = piece.astype(BF16)
    for d in range(1, ZN):
        zpush(4, d, wfin.at[q, z], wfin.at[q, z])

    def put(t, p):
        r = pl.ds(pl.multiple_of(t * W + (p // PC) * HR, 16), HR)
        c = pl.ds(pl.multiple_of(lax.rem(p, PC) * HC, LANES), HC)
        store(wfin.at[t, p], gproj_hbm.at[r, c], out_sem.at[t, p])

    for k in range(ZN):
        p = zpeer(k)
        if k:
            zwait(4, k, wfin.at[q, p])
        here = wfin.at[q, p]
        for d in range(1, JN):
            push(here, here, fs_sem.at[d, p], fr_sem.at[jme, p], jdev(jpeer(d)))
        push(here, here, hs_sem.at[jme, p], hr_sem.at[jme, p], sibling)
        put(q, p)
    for k in range(ZN):
        p = zpeer(k)
        for d in range(1, JN):
            j = jpeer(d)
            t = slot(j, core)
            here = wfin.at[t, p]
            arrive(here, fs_sem.at[d, p], fr_sem.at[j, p], jdev(j))
            push(here, here, hs_sem.at[j, p], hr_sem.at[j, p], sibling)
            put(t, p)
    for k in range(ZN):
        p = zpeer(k)
        for d in range(JN):
            j = jpeer(d)
            t = slot(j, other)
            arrive(wfin.at[t, p], hs_sem.at[j, p], hr_sem.at[j, p], sibling)
            put(t, p)
    for c, cond in sends:
        if cond is None:
            c.wait_send()
        else:
            pl.when(cond)(c.wait_send)
    for c in stores:
        c.wait()


def finish(gs_in, gt_in, gp_in, gs_out, gt_out, gp_out, low, wide, whole_sem, in_sem, out_sem):
    rows = low.shape[1]
    whole = [
        pltpu.make_async_copy(a, b, whole_sem.at[k])
        for k, (a, b) in enumerate([(gs_in, gs_out), (gt_in, gt_out)])
    ]
    loads = [
        pltpu.make_async_copy(gp_in.at[pl.ds(k * rows, rows), :], low.at[k], in_sem.at[k])
        for k in range(PARTS)
    ]
    stores = [
        pltpu.make_async_copy(wide.at[k], gp_out.at[pl.ds(k * rows, rows), :], out_sem.at[k])
        for k in range(PARTS)
    ]
    for c in loads + whole:
        c.start()
    for k in range(PARTS):
        loads[k].wait()
        wide[k] = low[k].astype(F32)
        stores[k].start()
    for c in whole + stores:
        c.wait()


def fused_device(RN, CN, PR, PC, sources, targets, projection, language, lang_allow, tile_allow):
    ZN, QN, JN = CN // YN, RN * YN, RN * YN // CORES
    B, D = sources.shape
    NL = lang_allow.shape[0]
    W = D // QN
    langs = language.reshape(-1, B)
    smem = pl.BlockSpec(memory_space=pltpu.SMEM)
    hbm = pl.BlockSpec(memory_space=pltpu.HBM)
    V = pltpu.VMEM
    S = pltpu.SemaphoreType.DMA
    piece = (ZN, W // PR, D // PC)
    grad_sources, grad_targets, grad_proj = pl.pallas_call(
        functools.partial(fused, RN, ZN, PR, PC),
        out_shape=(
            jax.ShapeDtypeStruct((B, D), BF16),
            jax.ShapeDtypeStruct((B, D), BF16),
            jax.ShapeDtypeStruct((D, D), BF16),
        ),
        in_specs=[hbm] * 5 + [smem],
        out_specs=(hbm,) * 3,
        scratch_shapes=[
            V((B, D), BF16),
            V((B, D), BF16),
            V((D, D), BF16),
            V(langs.shape, jnp.int32),
            V((NL, NL), jnp.int32),
            V((B, D), BF16),
            V((B, D), BF16),
            V((B, D), F32),
            V((B, D), F32),
            V((ZN, B, D), BF16),
            V((QN, B, D), BF16),
            V((NL, QN * B), BF16),
            V((ZN, B, QN * B), F32),
            V((ZN, B, QN * B), F32),
            V((QN, ZN * B, B), BF16),
            V((ZN, ZN, B), F32),
            V((ZN, B), F32),
            V((QN, 1, QN * B), F32),
            V((ZN, B, D), BF16),
            V((ZN, B, D), BF16),
            V((JN, B, D), F32),
            V((JN, B, D), F32),
            V((JN, B, D), BF16),
            V((JN, B, D), BF16),
            V((ZN, 1, B), F32),
            V((ZN, 1, B), F32),
            V((JN, 1, B), F32),
            V((JN, 1, B), F32),
            V((D, D), F32),
            V((JN, W, D), F32),
            V((JN, W, D), BF16),
            V((JN, W, D), BF16),
            V(piece, F32),
            V(piece, BF16),
            V(piece, BF16),
            V((QN, *piece), BF16),
            S((7,)),
            S((6, ZN)),
            S((6, ZN)),
            S((QN,)),
            S((QN,)),
            S((4, JN)),
            S((4, JN)),
            S((3, JN)),
            S((3, JN)),
            S((JN, ZN)),
            S((JN, ZN)),
            S((JN, ZN)),
            S((JN, ZN)),
            S((QN, ZN)),
            V((B, D), F32),
            V((1, B), F32),
            V((B, D), BF16),
            V((1, B), F32),
            V((B, D), F32),
            V((1, B), F32),
            S((5,)),
            S((2,)),
        ],
        compiler_params=pltpu.CompilerParams(
            collective_id=0, has_side_effects=True, vmem_limit_bytes=60 * 2**20
        ),
    )(sources, targets, projection, langs, lang_allow, tile_allow)
    rows = D // PARTS
    return pl.pallas_call(
        finish,
        out_shape=(
            jax.ShapeDtypeStruct((B, D), BF16),
            jax.ShapeDtypeStruct((B, D), BF16),
            jax.ShapeDtypeStruct((D, D), F32),
        ),
        in_specs=[hbm] * 3,
        out_specs=(hbm,) * 3,
        scratch_shapes=[
            V((PARTS, rows, D), BF16),
            V((PARTS, rows, D), F32),
            S((2,)),
            S((PARTS,)),
            S((PARTS,)),
        ],
        compiler_params=pltpu.CompilerParams(vmem_limit_bytes=60 * 2**20),
    )(grad_sources, grad_targets, grad_proj)


def embedded(inputs, projection):
    raw_proj = jnp.dot(inputs, projection, preferred_element_type=jnp.float32)
    length = jnp.sqrt(jnp.sum(raw_proj * raw_proj, axis=-1, keepdims=True) + 1e-06)
    return (raw_proj, length)


def permitted(row_index, col_index, language, lang_allow, tile_allow):
    tile_cols = jnp.take(tile_allow, col_index // TILE, axis=1)
    tile_ok = jnp.take(tile_cols, row_index // TILE, axis=0)
    row_lang = lax.dynamic_slice_in_dim(language, row_index[0], row_index.shape[0])
    col_lang = lax.dynamic_slice_in_dim(language, col_index[0], col_index.shape[0])
    lang_cols = jnp.take(lang_allow, col_lang, axis=1)
    pair_ok = jnp.take(lang_cols, row_lang, axis=0)
    return (tile_ok * pair_ok == 1) | (row_index[:, None] == col_index[None, :])


def backward_proj(inputs, raw_proj, length, upstream, projection):
    unit_vec = raw_proj / length
    dir_grad = (
        (upstream - unit_vec * jnp.sum(unit_vec * upstream, axis=-1, keepdims=True)) / length
    ).astype(jnp.bfloat16)
    grad_in = jnp.dot(dir_grad, projection.T, preferred_element_type=jnp.float32).astype(
        jnp.bfloat16
    )
    grad_weight = jnp.dot(inputs.T, dir_grad, preferred_element_type=jnp.float32)
    return (grad_in, grad_weight)


def per_device(sources, targets, projection, language, lang_allow, tile_allow):
    src_raw, src_len = embedded(sources, projection)
    tgt_raw, tgt_len = embedded(targets, projection)
    src_unit = (src_raw / src_len).astype(jnp.bfloat16)
    tgt_unit = (tgt_raw / tgt_len).astype(jnp.bfloat16)
    row_emb = lax.all_gather(src_unit, "col", axis=0, tiled=True)
    col_emb = lax.all_gather(tgt_unit, "row", axis=0, tiled=True)
    row_count = row_emb.shape[0]
    col_count = col_emb.shape[0]
    row_begin = lax.axis_index("row") * row_count
    col_begin = lax.axis_index("col") * col_count
    row_index = row_begin + jnp.arange(row_count)
    col_index = col_begin + jnp.arange(col_count)
    allowed = permitted(row_index, col_index, language, lang_allow, tile_allow)
    similar = jnp.dot(row_emb, col_emb.T, preferred_element_type=jnp.float32)
    diagonal = (row_index[:, None] == col_index[None, :]).astype(jnp.float32)
    logits = SCALE * (similar - MARGIN * diagonal)
    weights = jnp.where(allowed, jnp.exp(logits - SCALE), jnp.float32(0.0))
    row_part = jnp.sum(weights, axis=1)
    col_part = jnp.sum(weights, axis=0)
    row_total = lax.psum(row_part, "col")
    col_total = lax.psum(col_part, "row")
    row_lse = jnp.log(row_total) + SCALE
    col_lse = jnp.log(col_total) + SCALE
    soft_rows = jnp.where(allowed, jnp.exp(logits - row_lse[:, None]), jnp.float32(0.0))
    soft_cols = jnp.where(allowed, jnp.exp(logits - col_lse[None, :]), jnp.float32(0.0))
    logit_grad = (SCALE * (0.5 * (soft_rows + soft_cols) - diagonal)).astype(jnp.bfloat16)
    src_terms = jnp.dot(logit_grad, col_emb, preferred_element_type=jnp.float32)
    src_grad = lax.psum_scatter(src_terms, "col", scatter_dimension=0, tiled=True)
    tgt_terms = lax.dot_general(
        logit_grad, row_emb, (((0,), (0,)), ((), ())), preferred_element_type=jnp.float32
    )
    tgt_grad = lax.psum_scatter(tgt_terms, "row", scatter_dimension=0, tiled=True)
    grad_sources, weight_src = backward_proj(sources, src_raw, src_len, src_grad, projection)
    grad_targets, weight_tgt = backward_proj(targets, tgt_raw, tgt_len, tgt_grad, projection)
    grad_proj = lax.psum(weight_src + weight_tgt, ("row", "col"))
    return (grad_sources, grad_targets, grad_proj)


def pieces(ZN, W, D):
    for PR in (1, 2, 4):
        if ZN % PR == 0 and W % (16 * PR) == 0 and D % (LANES * (ZN // PR)) == 0:
            return PR, ZN // PR
    return None


def solution(mesh):
    RN, CN = mesh.shape["row"], mesh.shape["col"]

    def device(sources, targets, projection, language, lang_allow, tile_allow):
        B, D = sources.shape
        split = None
        if CN % YN == 0 and RN % CORES == 0 and D % (16 * RN * YN) == 0 and B == LANES and RN * CN <= 64:
            split = pieces(CN // YN, D // (RN * YN), D)
        args = (sources, targets, projection, language, lang_allow, tile_allow)
        if split is None:
            return per_device(*args)
        return fused_device(RN, CN, *split, *args)

    return jax.shard_map(
        device,
        mesh=mesh,
        in_specs=(P(("row", "col"), None), P(("col", "row"), None), P(), P(), P(), P()),
        out_specs=(P(("row", "col"), None), P(("col", "row"), None), P()),
        check_vma=False,
    )
```

```python
import functools

import jax
import jax.numpy as jnp
from jax import lax
from jax.experimental import pallas as pl
from jax.experimental.pallas import tpu as pltpu
from jax.sharding import PartitionSpec as P

TILE = 512
LANES = 128
SCALE = 20.0
MARGIN = 0.3
YN = 2
CORES = 2
PARTS = 4
BF16 = jnp.bfloat16
F32 = jnp.float32
MESH = pl.DeviceIdType.MESH


def mm(a, b, ca, cb):
    return lax.dot_general(a, b, (((ca,), (cb,)), ((), ())), preferred_element_type=F32)


def fused(
    RN, ZN, PR, PC,
    src_hbm, tgt_hbm, proj_hbm, lang_hbm, allow_hbm, tile_ref,
    gsrc_hbm, gtgt_hbm, gproj_hbm,
    src_ref, tgt_ref, proj_ref, lang_ref, allow_ref, gsrc_ref, gtgt_ref,
    sraw, traw, sun, tun, lang_cols, mask, e_ref, g_ref,
    rowx, row_inv, colx, ssend, srecv, tcs, tcr, tsend, trecv, salong, ralong, talong, qalong,
    w_ref, wcr, wsend, wrecv, zpart, zsend, zrecv, wfin,
    loc_sem, zs_sem, zr_sem, qs_sem, qr_sem, js_sem, jr_sem, cs_sem, cr_sem,
    fs_sem, fr_sem, hs_sem, hr_sem, out_sem,
    hold, hold_along, passed, passed_along, src_acc, along_acc, rs_sem, rr_sem,
):
    QN = RN * YN
    XN = RN // CORES
    JN = XN * YN
    CN = ZN * YN
    B, D = src_ref.shape
    cols = QN * B
    W = D // QN
    HR, HC = W // PR, D // PC
    row = lax.axis_index("row")
    col = lax.axis_index("col")
    y = lax.rem(col, YN)
    z = col // YN
    q = y * RN + row
    core = lax.rem(row, CORES)
    other = 1 - core
    jme = y * XN + row // CORES

    def zpeer(d):
        return lax.rem(z + d, ZN)

    def qpeer(d):
        return lax.rem(q + d, QN)

    def jpeer(d):
        return lax.rem(jme + d, JN)

    def slot(j, c):
        return (j // XN) * RN + lax.rem(j, XN) * CORES + c

    def zdev(t):
        return (row, t * YN + y)

    def qdev(t):
        return (lax.rem(t, RN), z * YN + t // RN)

    def jdev(j):
        return (lax.rem(j, XN) * CORES + core, z * YN + j // XN)

    sibling = (row + 1 - 2 * core, col)

    sends = []

    def push(src, dst, s_sem, r_sem, dev, cond=None):
        c = pltpu.make_async_remote_copy(src, dst, s_sem, r_sem, device_id=dev, device_id_type=MESH)
        if cond is None:
            c.start()
        else:
            pl.when(cond)(c.start)
        sends.append((c, cond))

    def arrive(buf, s_sem, r_sem, dev):
        pltpu.make_async_remote_copy(
            buf, buf, s_sem, r_sem, device_id=dev, device_id_type=MESH
        ).wait_recv()

    last = ZN - 1
    relays = ZN == 4

    def far(t):
        return ((z == 0) & (t == last)) | ((z == last) & (t == 0))

    def middle(t):
        return ((z == last - 1) & (t == 0)) | ((z == 1) & (t == last))

    def no(c):
        return jnp.logical_not(c)

    opposite = last - z
    scatter_c = 2 * z + 1 - 5 * (z // 2)
    scatter_b = last - scatter_c

    def zpush_to(k, s, src, dst, cond=None):
        push(src, dst, zs_sem.at[k, s], zr_sem.at[k, z], zdev(s), cond)

    def zpush(k, d, src, dst, cond=None):
        push(src, dst, zs_sem.at[k, d], zr_sem.at[k, z], zdev(zpeer(d)), cond)

    def zwait(k, d, buf):
        t = zpeer(d)
        arrive(buf, zs_sem.at[k, d], zr_sem.at[k, t], zdev(t))

    def jpush(k, d, src, dst):
        push(src, dst, js_sem.at[k, d], jr_sem.at[k, jme], jdev(jpeer(d)))

    def jwait(k, d, buf):
        j = jpeer(d)
        arrive(buf, js_sem.at[k, d], jr_sem.at[k, j], jdev(j))

    def cpush(k, j, src, dst):
        push(src, dst, cs_sem.at[k, j], cr_sem.at[k, j], sibling)

    def cwait(k, j, buf):
        arrive(buf, cs_sem.at[k, j], cr_sem.at[k, j], sibling)

    barrier = pltpu.get_barrier_semaphore()
    for d in range(1, ZN):
        pl.semaphore_signal(barrier, inc=1, device_id=zdev(zpeer(d)), device_id_type=MESH)
    for d in range(1, QN):
        pl.semaphore_signal(barrier, inc=1, device_id=qdev(qpeer(d)), device_id_type=MESH)
    loads = [
        pltpu.make_async_copy(a, b, loc_sem.at[k])
        for k, (a, b) in enumerate(
            [
                (src_hbm, src_ref), (proj_hbm, proj_ref), (tgt_hbm, tgt_ref),
                (lang_hbm, lang_ref), (allow_hbm, allow_ref),
            ]
        )
    ]
    for c in loads:
        c.start()

    stores = []

    def store(src, dst, sem):
        c = pltpu.make_async_copy(src, dst, sem)
        c.start()
        stores.append(c)

    def embed(inp, raw):
        r = mm(inp[...], proj_ref[...], 1, 0)
        raw[...] = r
        length = jnp.sqrt(jnp.sum(r * r, axis=-1, keepdims=True) + 1e-06)
        return (r / length).astype(BF16)

    loads[0].wait()
    loads[1].wait()
    sun[z] = embed(src_ref, sraw)
    pl.semaphore_wait(barrier, ZN + QN - 2)
    at_end = (z == 0) | (z == last)
    if relays:
        for s in (scatter_b, scatter_c):
            zpush_to(0, s, sun.at[z], sun.at[z])
        across, _ = sends.pop()
    else:
        for d in range(1, ZN):
            zpush(0, d, sun.at[z], sun.at[z])
    loads[2].wait()
    tun[q] = embed(tgt_ref, traw)
    for d in range(1, JN):
        jpush(0, d, tun.at[q], tun.at[q])
    cpush(0, jme, tun.at[q], tun.at[q])

    loads[3].wait()
    loads[4].wait()
    NL = allow_ref.shape[0]
    kind = lax.broadcasted_iota(jnp.int32, (NL, B), 0)
    allow = allow_ref[...].astype(F32).astype(BF16)

    def one_hot(block):
        return jnp.where(kind == lang_ref[pl.ds(block, 1), :], 1.0, 0.0).astype(BF16)

    for t in range(QN):
        lang_cols[:, t * B : (t + 1) * B] = mm(allow, one_hot(z * QN + t), 1, 0).astype(BF16)

    def diagonal(s):
        rows = lax.broadcasted_iota(jnp.int32, (B, cols), 0) + (row * CN + s * YN + y) * B
        colid = lax.broadcasted_iota(jnp.int32, (B, cols), 1) + z * cols
        return rows == colid

    def mask_step(s, c):
        sb = row * CN + s * YN + y
        ok = mm(one_hot(sb), lang_cols[...], 0, 0)
        for t in range(QN):
            tile_ok = tile_ref[sb * B // TILE, (z * QN + t) * B // TILE]
            part = ok[:, t * B : (t + 1) * B]
            mask[s, :, t * B : (t + 1) * B] = jnp.where(tile_ok == 1, part, 0.0)
        return c

    lax.fori_loop(0, ZN, mask_step, 0)

    for d in range(1, JN):
        j = jpeer(d)
        t = slot(j, core)
        jwait(0, d, tun.at[t])
        cpush(0, j, tun.at[t], tun.at[t])
    if relays:
        across.wait_send()
        zpush_to(0, opposite, sun.at[z], sun.at[z], no(at_end))
    for d in range(JN):
        j = jpeer(d)
        cwait(0, j, tun.at[slot(j, other)])

    colx[q] = jnp.zeros((1, cols), F32)

    def totals(s):
        diag = diagonal(s)
        sim = mm(sun[s], tun[...].reshape(cols, D), 1, 1)
        logits = SCALE * (sim - jnp.where(diag, MARGIN, 0.0))
        e = jnp.where(diag | (mask[s] > 0.5), jnp.exp(logits - SCALE), 0.0)
        e_ref[s] = e
        part = e[:, :LANES]
        for t in range(1, cols // LANES):
            part += e[:, t * LANES : (t + 1) * LANES]
        rowx[z, pl.ds(s, 1), :] = jnp.sum(part.T, axis=0, keepdims=True)
        colx[q] += jnp.sum(e, axis=0, keepdims=True)

    totals(z)
    if relays:
        s = scatter_c
        pl.when(no(at_end))(
            lambda: arrive(sun.at[s], zs_sem.at[0, s], zr_sem.at[0, s], zdev(s))
        )
        push(sun.at[s], sun.at[s], rs_sem.at[2], zr_sem.at[0, s], zdev(last - s), no(at_end))
        first = 1 + lax.rem(z, 2)
        final = last * (1 - z // 2)
        order = [first, last * 2 - z - first - final, final]
    else:
        order = [zpeer(d) for d in range(1, ZN)]

    def take(s):
        arrive(sun.at[s], zs_sem.at[0, 1], zr_sem.at[0, s], zdev(s))

    for k, s in enumerate(order):
        if relays and k == len(order) - 1:
            pl.when(no(middle(s)))(functools.partial(take, s))
        else:
            take(s)
        totals(s)
    for d in range(1, ZN):
        zpush(1, d, rowx.at[z], rowx.at[z])
    for d in range(1, QN):
        push(colx.at[q], colx.at[q], qs_sem.at[d], qr_sem.at[q], qdev(qpeer(d)))
    for d in range(1, ZN):
        zwait(1, d, rowx.at[zpeer(d)])
    for d in range(1, QN):
        t = qpeer(d)
        arrive(colx.at[t], qs_sem.at[d], qr_sem.at[t], qdev(t))
    row_inv[...] = (0.5 * SCALE) / jnp.sum(rowx[...], axis=0)
    col_inv = (0.5 * SCALE) / jnp.sum(colx[...], axis=0)

    def grad_block(s):
        inv = jnp.broadcast_to(row_inv[pl.ds(s, 1), :], (B, B)).T[:, :1]
        g = e_ref[s] * (inv + col_inv) - jnp.where(diagonal(s), SCALE, 0.0)
        g = g.astype(BF16)
        for t in range(QN):
            g_ref[t, pl.ds(pl.multiple_of(s * B, B), B), :] = g[:, t * B : (t + 1) * B]
        return mm(g, tun[...].reshape(cols, D), 1, 0)

    def split(part, unit):
        u = unit.astype(F32)
        along = jnp.sum(part * u, axis=-1, keepdims=True)
        rest = part - along * u
        return rest.astype(BF16), jnp.broadcast_to(along, (B, B)).T[:1, :]

    def along_unit(along, unit):
        return jnp.broadcast_to(along, (B, B)).T[:, :1] * unit.astype(F32)

    def source_part(s):
        part = grad_block(s)
        u = sun[s].astype(F32)
        along = jnp.sum(part * u, axis=-1, keepdims=True)
        return part - along * u, jnp.broadcast_to(along, (B, B)).T[:1, :]

    def send_sources(s, cond=None):
        zpush_to(2, s, ssend.at[s], srecv.at[z], cond)
        zpush_to(5, s, salong.at[s], ralong.at[z], cond)

    for s in (opposite, scatter_b, scatter_c) if relays else [zpeer(d) for d in range(1, ZN)]:
        rest, along = source_part(s)
        ssend[s] = rest.astype(BF16)
        salong[s] = along
        if not relays:
            send_sources(s)
        elif s is opposite:
            send_sources(s, no(at_end))
            by = zdev(z + 1 - 2 * lax.rem(z, 2))
            push(salong.at[s], passed_along, rs_sem.at[1], rr_sem.at[1], by, at_end)
            push(ssend.at[s], passed, rs_sem.at[0], rr_sem.at[0], by, at_end)
            to_pass, _ = sends.pop()
        elif s is scatter_b:
            send_sources(s, no(at_end))
        else:
            hold[...] = rest
            hold_along[...] = along
    src_grad = grad_block(z)

    def tgt_part(t):
        return mm(g_ref[t], sun[...].reshape(ZN * B, D), 0, 0)

    for d in range(1, JN + 1):
        j = jpeer(d)
        tcs[j] = tgt_part(slot(j, other))
        cpush(1, j, tcs.at[j], tcr.at[j])
    if relays:
        s = scatter_c

        @pl.when(no(at_end))
        def _():
            dev = zdev(opposite)
            arrive(passed, rs_sem.at[0], rr_sem.at[0], dev)
            arrive(passed_along, rs_sem.at[1], rr_sem.at[1], dev)
            ssend[s] = (hold[...] + passed[...].astype(F32)).astype(BF16)
            salong[s] = hold_along[...] + passed_along[...]

        pl.when(at_end)(to_pass.wait_send)
        send_sources(scatter_b, at_end)
        send_sources(s)
    for d in range(1, JN):
        j = jpeer(d)
        t = slot(j, core)
        part = tgt_part(t)
        cwait(1, j, tcr.at[j])
        rest, along = split(part + tcr[j], tun[t])
        tsend[j] = rest
        talong[j] = along
        jpush(1, d, tsend.at[j], trecv.at[jme])
        jpush(2, d, talong.at[j], qalong.at[jme])
    tgt_grad = tgt_part(q)
    cwait(1, jme, tcr.at[jme])
    tgt_grad += tcr[jme]

    def direction(raw, grad):
        r = raw[...]
        length = jnp.sqrt(jnp.sum(r * r, axis=-1, keepdims=True) + 1e-06)
        unit = r / length
        return (
            (grad - unit * jnp.sum(unit * grad, axis=-1, keepdims=True)) / length
        ).astype(BF16)

    along = jnp.zeros((1, B), F32)
    for d in range(1, JN):
        j = jpeer(d)
        jwait(1, d, trecv.at[j])
        jwait(2, d, qalong.at[j])
        tgt_grad += trecv[j].astype(F32)
        along += qalong[j]
    tgt_grad += along_unit(along, tun[q])
    tgt_dir = direction(traw, tgt_grad)
    w_ref[...] = mm(tgt_ref[...], tgt_dir, 0, 0)
    gtgt_ref[...] = mm(tgt_dir, proj_ref[...], 1, 1).astype(BF16)
    store(gtgt_ref, gtgt_hbm, loc_sem.at[5])

    src_acc[...] = src_grad
    along_acc[...] = jnp.zeros((1, B), F32)
    for d in range(1, ZN):
        s = zpeer(d)

        def add(d=d, s=s):
            zwait(2, d, srecv.at[s])
            zwait(5, d, ralong.at[s])
            src_acc[...] += srecv[s].astype(F32)
            along_acc[...] += ralong[s]

        if relays:
            pl.when(no(far(s)))(add)
        else:
            add()
    src_grad = src_acc[...] + along_unit(along_acc[...], sun[z])
    src_dir = direction(sraw, src_grad)

    w_ref[...] += mm(src_ref[...], src_dir, 0, 0)

    def rows_of(t):
        return pl.ds(pl.multiple_of(t * W, 16), W)

    for d in range(1, JN + 1):
        j = jpeer(d)
        cpush(2, j, w_ref.at[rows_of(slot(j, other))], wcr.at[j])
    gsrc_ref[...] = mm(src_dir, proj_ref[...], 1, 1).astype(BF16)
    store(gsrc_ref, gsrc_hbm, loc_sem.at[6])
    for d in range(1, JN):
        j = jpeer(d)
        cwait(2, j, wcr.at[j])
        wsend[j] = (w_ref[rows_of(slot(j, core)), :] + wcr[j]).astype(BF16)
        jpush(3, d, wsend.at[j], wrecv.at[jme])
    cwait(2, jme, wcr.at[jme])
    total = w_ref[rows_of(q), :] + wcr[jme]
    for d in range(1, JN):
        j = jpeer(d)
        jwait(3, d, wrecv.at[j])
        total += wrecv[j].astype(F32)
    for p in range(ZN):
        a, b = p // PC, p % PC
        zpart[p] = total[a * HR : (a + 1) * HR, b * HC : (b + 1) * HC]
    for d in range(1, ZN):
        s = zpeer(d)
        zsend[s] = zpart[s].astype(BF16)
        zpush(3, d, zsend.at[s], zrecv.at[z])
    piece = zpart[z]
    for d in range(1, ZN):
        s = zpeer(d)
        zwait(3, d, zrecv.at[s])
        piece += zrecv[s].astype(F32)
    wfin[q, z] = piece.astype(BF16)
    for d in range(1, ZN):
        zpush(4, d, wfin.at[q, z], wfin.at[q, z])

    def put(t, p):
        r = pl.ds(pl.multiple_of(t * W + (p // PC) * HR, 16), HR)
        c = pl.ds(pl.multiple_of(lax.rem(p, PC) * HC, LANES), HC)
        store(wfin.at[t, p], gproj_hbm.at[r, c], out_sem.at[t, p])

    for k in range(ZN):
        p = zpeer(k)
        if k:
            zwait(4, k, wfin.at[q, p])
        here = wfin.at[q, p]
        for d in range(1, JN):
            push(here, here, fs_sem.at[d, p], fr_sem.at[jme, p], jdev(jpeer(d)))
        push(here, here, hs_sem.at[jme, p], hr_sem.at[jme, p], sibling)
        put(q, p)
    for k in range(ZN):
        p = zpeer(k)
        for d in range(1, JN):
            j = jpeer(d)
            t = slot(j, core)
            here = wfin.at[t, p]
            arrive(here, fs_sem.at[d, p], fr_sem.at[j, p], jdev(j))
            push(here, here, hs_sem.at[j, p], hr_sem.at[j, p], sibling)
            put(t, p)
    for k in range(ZN):
        p = zpeer(k)
        for d in range(JN):
            j = jpeer(d)
            t = slot(j, other)
            arrive(wfin.at[t, p], hs_sem.at[j, p], hr_sem.at[j, p], sibling)
            put(t, p)
    for c, cond in sends:
        if cond is None:
            c.wait_send()
        else:
            pl.when(cond)(c.wait_send)
    for c in stores:
        c.wait()


def finish(gs_in, gt_in, gp_in, gs_out, gt_out, gp_out, low, wide, held, whole_sem, in_sem, out_sem):
    rows = low.shape[1]
    whole_in = [
        pltpu.make_async_copy(a, held.at[k], whole_sem.at[k]) for k, a in enumerate([gs_in, gt_in])
    ]
    whole_out = [
        pltpu.make_async_copy(held.at[k], b, whole_sem.at[2 + k])
        for k, b in enumerate([gs_out, gt_out])
    ]
    loads = [
        pltpu.make_async_copy(gp_in.at[pl.ds(k * rows, rows), :], low.at[k], in_sem.at[k])
        for k in range(PARTS)
    ]
    stores = [
        pltpu.make_async_copy(wide.at[k], gp_out.at[pl.ds(k * rows, rows), :], out_sem.at[k])
        for k in range(PARTS)
    ]
    for c in loads + whole_in:
        c.start()
    for k in range(PARTS):
        loads[k].wait()
        wide[k] = low[k].astype(F32)
        stores[k].start()
    for k in range(2):
        whole_in[k].wait()
        whole_out[k].start()
    for c in whole_out + stores:
        c.wait()


def fused_device(RN, CN, PR, PC, sources, targets, projection, language, lang_allow, tile_allow):
    ZN, QN, JN = CN // YN, RN * YN, RN * YN // CORES
    B, D = sources.shape
    NL = lang_allow.shape[0]
    W = D // QN
    langs = language.reshape(-1, B)
    smem = pl.BlockSpec(memory_space=pltpu.SMEM)
    hbm = pl.BlockSpec(memory_space=pltpu.HBM)
    V = pltpu.VMEM
    S = pltpu.SemaphoreType.DMA
    piece = (ZN, W // PR, D // PC)
    grad_sources, grad_targets, grad_proj = pl.pallas_call(
        functools.partial(fused, RN, ZN, PR, PC),
        out_shape=(
            jax.ShapeDtypeStruct((B, D), BF16),
            jax.ShapeDtypeStruct((B, D), BF16),
            jax.ShapeDtypeStruct((D, D), BF16),
        ),
        in_specs=[hbm] * 5 + [smem],
        out_specs=(hbm,) * 3,
        scratch_shapes=[
            V((B, D), BF16),
            V((B, D), BF16),
            V((D, D), BF16),
            V(langs.shape, jnp.int32),
            V((NL, NL), jnp.int32),
            V((B, D), BF16),
            V((B, D), BF16),
            V((B, D), F32),
            V((B, D), F32),
            V((ZN, B, D), BF16),
            V((QN, B, D), BF16),
            V((NL, QN * B), BF16),
            V((ZN, B, QN * B), F32),
            V((ZN, B, QN * B), F32),
            V((QN, ZN * B, B), BF16),
            V((ZN, ZN, B), F32),
            V((ZN, B), F32),
            V((QN, 1, QN * B), F32),
            V((ZN, B, D), BF16),
            V((ZN, B, D), BF16),
            V((JN, B, D), F32),
            V((JN, B, D), F32),
            V((JN, B, D), BF16),
            V((JN, B, D), BF16),
            V((ZN, 1, B), F32),
            V((ZN, 1, B), F32),
            V((JN, 1, B), F32),
            V((JN, 1, B), F32),
            V((D, D), F32),
            V((JN, W, D), F32),
            V((JN, W, D), BF16),
            V((JN, W, D), BF16),
            V(piece, F32),
            V(piece, BF16),
            V(piece, BF16),
            V((QN, *piece), BF16),
            S((7,)),
            S((6, ZN)),
            S((6, ZN)),
            S((QN,)),
            S((QN,)),
            S((4, JN)),
            S((4, JN)),
            S((3, JN)),
            S((3, JN)),
            S((JN, ZN)),
            S((JN, ZN)),
            S((JN, ZN)),
            S((JN, ZN)),
            S((QN, ZN)),
            V((B, D), F32),
            V((1, B), F32),
            V((B, D), BF16),
            V((1, B), F32),
            V((B, D), F32),
            V((1, B), F32),
            S((5,)),
            S((2,)),
        ],
        compiler_params=pltpu.CompilerParams(
            collective_id=0, has_side_effects=True, vmem_limit_bytes=60 * 2**20
        ),
    )(sources, targets, projection, langs, lang_allow, tile_allow)
    rows = D // PARTS
    return pl.pallas_call(
        finish,
        out_shape=(
            jax.ShapeDtypeStruct((B, D), BF16),
            jax.ShapeDtypeStruct((B, D), BF16),
            jax.ShapeDtypeStruct((D, D), F32),
        ),
        in_specs=[hbm] * 3,
        out_specs=(hbm,) * 3,
        scratch_shapes=[
            V((PARTS, rows, D), BF16),
            V((PARTS, rows, D), F32),
            V((2, B, D), BF16),
            S((4,)),
            S((PARTS,)),
            S((PARTS,)),
        ],
        compiler_params=pltpu.CompilerParams(vmem_limit_bytes=60 * 2**20),
    )(grad_sources, grad_targets, grad_proj)


def embedded(inputs, projection):
    raw_proj = jnp.dot(inputs, projection, preferred_element_type=jnp.float32)
    length = jnp.sqrt(jnp.sum(raw_proj * raw_proj, axis=-1, keepdims=True) + 1e-06)
    return (raw_proj, length)


def permitted(row_index, col_index, language, lang_allow, tile_allow):
    tile_cols = jnp.take(tile_allow, col_index // TILE, axis=1)
    tile_ok = jnp.take(tile_cols, row_index // TILE, axis=0)
    row_lang = lax.dynamic_slice_in_dim(language, row_index[0], row_index.shape[0])
    col_lang = lax.dynamic_slice_in_dim(language, col_index[0], col_index.shape[0])
    lang_cols = jnp.take(lang_allow, col_lang, axis=1)
    pair_ok = jnp.take(lang_cols, row_lang, axis=0)
    return (tile_ok * pair_ok == 1) | (row_index[:, None] == col_index[None, :])


def backward_proj(inputs, raw_proj, length, upstream, projection):
    unit_vec = raw_proj / length
    dir_grad = (
        (upstream - unit_vec * jnp.sum(unit_vec * upstream, axis=-1, keepdims=True)) / length
    ).astype(jnp.bfloat16)
    grad_in = jnp.dot(dir_grad, projection.T, preferred_element_type=jnp.float32).astype(
        jnp.bfloat16
    )
    grad_weight = jnp.dot(inputs.T, dir_grad, preferred_element_type=jnp.float32)
    return (grad_in, grad_weight)


def per_device(sources, targets, projection, language, lang_allow, tile_allow):
    src_raw, src_len = embedded(sources, projection)
    tgt_raw, tgt_len = embedded(targets, projection)
    src_unit = (src_raw / src_len).astype(jnp.bfloat16)
    tgt_unit = (tgt_raw / tgt_len).astype(jnp.bfloat16)
    row_emb = lax.all_gather(src_unit, "col", axis=0, tiled=True)
    col_emb = lax.all_gather(tgt_unit, "row", axis=0, tiled=True)
    row_count = row_emb.shape[0]
    col_count = col_emb.shape[0]
    row_begin = lax.axis_index("row") * row_count
    col_begin = lax.axis_index("col") * col_count
    row_index = row_begin + jnp.arange(row_count)
    col_index = col_begin + jnp.arange(col_count)
    allowed = permitted(row_index, col_index, language, lang_allow, tile_allow)
    similar = jnp.dot(row_emb, col_emb.T, preferred_element_type=jnp.float32)
    diagonal = (row_index[:, None] == col_index[None, :]).astype(jnp.float32)
    logits = SCALE * (similar - MARGIN * diagonal)
    weights = jnp.where(allowed, jnp.exp(logits - SCALE), jnp.float32(0.0))
    row_part = jnp.sum(weights, axis=1)
    col_part = jnp.sum(weights, axis=0)
    row_total = lax.psum(row_part, "col")
    col_total = lax.psum(col_part, "row")
    row_lse = jnp.log(row_total) + SCALE
    col_lse = jnp.log(col_total) + SCALE
    soft_rows = jnp.where(allowed, jnp.exp(logits - row_lse[:, None]), jnp.float32(0.0))
    soft_cols = jnp.where(allowed, jnp.exp(logits - col_lse[None, :]), jnp.float32(0.0))
    logit_grad = (SCALE * (0.5 * (soft_rows + soft_cols) - diagonal)).astype(jnp.bfloat16)
    src_terms = jnp.dot(logit_grad, col_emb, preferred_element_type=jnp.float32)
    src_grad = lax.psum_scatter(src_terms, "col", scatter_dimension=0, tiled=True)
    tgt_terms = lax.dot_general(
        logit_grad, row_emb, (((0,), (0,)), ((), ())), preferred_element_type=jnp.float32
    )
    tgt_grad = lax.psum_scatter(tgt_terms, "row", scatter_dimension=0, tiled=True)
    grad_sources, weight_src = backward_proj(sources, src_raw, src_len, src_grad, projection)
    grad_targets, weight_tgt = backward_proj(targets, tgt_raw, tgt_len, tgt_grad, projection)
    grad_proj = lax.psum(weight_src + weight_tgt, ("row", "col"))
    return (grad_sources, grad_targets, grad_proj)


def pieces(ZN, W, D):
    for PR in (1, 2, 4):
        if ZN % PR == 0 and W % (16 * PR) == 0 and D % (LANES * (ZN // PR)) == 0:
            return PR, ZN // PR
    return None


def solution(mesh):
    RN, CN = mesh.shape["row"], mesh.shape["col"]

    def device(sources, targets, projection, language, lang_allow, tile_allow):
        B, D = sources.shape
        split = None
        if CN % YN == 0 and RN % CORES == 0 and D % (16 * RN * YN) == 0 and B == LANES and RN * CN <= 64:
            split = pieces(CN // YN, D // (RN * YN), D)
        args = (sources, targets, projection, language, lang_allow, tile_allow)
        if split is None:
            return per_device(*args)
        return fused_device(RN, CN, *split, *args)

    return jax.shard_map(
        device,
        mesh=mesh,
        in_specs=(P(("row", "col"), None), P(("col", "row"), None), P(), P(), P(), P()),
        out_specs=(P(("row", "col"), None), P(("col", "row"), None), P()),
        check_vma=False,
    )
```

```python
import functools

import jax
import jax.numpy as jnp
from jax import lax
from jax.experimental import pallas as pl
from jax.experimental.pallas import tpu as pltpu
from jax.sharding import PartitionSpec as P

TILE = 512
LANES = 128
SCALE = 20.0
MARGIN = 0.3
YN = 2
CORES = 2
PARTS = 4
BF16 = jnp.bfloat16
F32 = jnp.float32
MESH = pl.DeviceIdType.MESH


def mm(a, b, ca, cb):
    return lax.dot_general(a, b, (((ca,), (cb,)), ((), ())), preferred_element_type=F32)


def fused(
    RN, ZN, PR, PC,
    src_hbm, tgt_hbm, proj_hbm, lang_hbm, allow_hbm, tile_ref,
    gsrc_hbm, gtgt_hbm, gproj_hbm,
    src_ref, tgt_ref, proj_ref, lang_ref, allow_ref, gsrc_ref, gtgt_ref,
    sraw, traw, sun, tun, lang_cols, mask, e_ref, g_ref,
    rowx, row_inv, colx, ssend, srecv, tcs, tcr, tsend, trecv, salong, ralong, talong, qalong,
    w_ref, wcs, wcr, wsend, wrecv, zpart, zsend, zrecv, wfin,
    loc_sem, zs_sem, zr_sem, qs_sem, qr_sem, js_sem, jr_sem, cs_sem, cr_sem,
    fs_sem, fr_sem, hs_sem, hr_sem, out_sem,
    hold, hold_along, passed, passed_along, src_acc, along_acc, rs_sem, rr_sem,
):
    QN = RN * YN
    XN = RN // CORES
    JN = XN * YN
    CN = ZN * YN
    B, D = src_ref.shape
    cols = QN * B
    W = D // QN
    HR, HC = W // PR, D // PC
    row = lax.axis_index("row")
    col = lax.axis_index("col")
    y = lax.rem(col, YN)
    z = col // YN
    q = y * RN + row
    core = lax.rem(row, CORES)
    other = 1 - core
    jme = y * XN + row // CORES

    def zpeer(d):
        return lax.rem(z + d, ZN)

    def qpeer(d):
        return lax.rem(q + d, QN)

    def jpeer(d):
        return lax.rem(jme + d, JN)

    def slot(j, c):
        return (j // XN) * RN + lax.rem(j, XN) * CORES + c

    def zdev(t):
        return (row, t * YN + y)

    def qdev(t):
        return (lax.rem(t, RN), z * YN + t // RN)

    def jdev(j):
        return (lax.rem(j, XN) * CORES + core, z * YN + j // XN)

    sibling = (row + 1 - 2 * core, col)

    sends = []

    def push(src, dst, s_sem, r_sem, dev, cond=None):
        c = pltpu.make_async_remote_copy(src, dst, s_sem, r_sem, device_id=dev, device_id_type=MESH)
        if cond is None:
            c.start()
        else:
            pl.when(cond)(c.start)
        sends.append((c, cond))

    def arrive(buf, s_sem, r_sem, dev):
        pltpu.make_async_remote_copy(
            buf, buf, s_sem, r_sem, device_id=dev, device_id_type=MESH
        ).wait_recv()

    last = ZN - 1
    relays = ZN == 4

    def far(t):
        return ((z == 0) & (t == last)) | ((z == last) & (t == 0))

    def middle(t):
        return ((z == last - 1) & (t == 0)) | ((z == 1) & (t == last))

    def no(c):
        return jnp.logical_not(c)

    opposite = last - z
    scatter_c = 2 * z + 1 - 5 * (z // 2)
    scatter_b = last - scatter_c

    def zpush_to(k, s, src, dst, cond=None):
        push(src, dst, zs_sem.at[k, s], zr_sem.at[k, z], zdev(s), cond)

    def zpush(k, d, src, dst, cond=None):
        push(src, dst, zs_sem.at[k, d], zr_sem.at[k, z], zdev(zpeer(d)), cond)

    def zwait(k, d, buf):
        t = zpeer(d)
        arrive(buf, zs_sem.at[k, d], zr_sem.at[k, t], zdev(t))

    def jpush(k, d, src, dst):
        push(src, dst, js_sem.at[k, d], jr_sem.at[k, jme], jdev(jpeer(d)))

    def jwait(k, d, buf):
        j = jpeer(d)
        arrive(buf, js_sem.at[k, d], jr_sem.at[k, j], jdev(j))

    def cpush(k, j, src, dst):
        push(src, dst, cs_sem.at[k, j], cr_sem.at[k, j], sibling)

    def cwait(k, j, buf):
        arrive(buf, cs_sem.at[k, j], cr_sem.at[k, j], sibling)

    barrier = pltpu.get_barrier_semaphore()
    for d in range(1, ZN):
        pl.semaphore_signal(barrier, inc=1, device_id=zdev(zpeer(d)), device_id_type=MESH)
    for d in range(1, QN):
        pl.semaphore_signal(barrier, inc=1, device_id=qdev(qpeer(d)), device_id_type=MESH)
    loads = [
        pltpu.make_async_copy(a, b, loc_sem.at[k])
        for k, (a, b) in enumerate(
            [
                (src_hbm, src_ref), (proj_hbm, proj_ref), (tgt_hbm, tgt_ref),
                (lang_hbm, lang_ref), (allow_hbm, allow_ref),
            ]
        )
    ]
    for c in loads:
        c.start()

    stores = []

    def store(src, dst, sem):
        c = pltpu.make_async_copy(src, dst, sem)
        c.start()
        stores.append(c)

    def embed(inp, raw):
        r = mm(inp[...], proj_ref[...], 1, 0)
        raw[...] = r
        length = jnp.sqrt(jnp.sum(r * r, axis=-1, keepdims=True) + 1e-06)
        return (r / length).astype(BF16)

    loads[0].wait()
    loads[1].wait()
    sun[z] = embed(src_ref, sraw)
    pl.semaphore_wait(barrier, ZN + QN - 2)
    at_end = (z == 0) | (z == last)
    if relays:
        for s in (scatter_b, scatter_c):
            zpush_to(0, s, sun.at[z], sun.at[z])
        across, _ = sends.pop()
    else:
        for d in range(1, ZN):
            zpush(0, d, sun.at[z], sun.at[z])
    loads[2].wait()
    tun[q] = embed(tgt_ref, traw)
    for d in range(1, JN):
        jpush(0, d, tun.at[q], tun.at[q])
    cpush(0, jme, tun.at[q], tun.at[q])

    loads[3].wait()
    loads[4].wait()
    NL = allow_ref.shape[0]
    kind = lax.broadcasted_iota(jnp.int32, (NL, B), 0)
    allow = allow_ref[...].astype(F32).astype(BF16)

    def one_hot(block):
        return jnp.where(kind == lang_ref[pl.ds(block, 1), :], 1.0, 0.0).astype(BF16)

    for t in range(QN):
        lang_cols[:, t * B : (t + 1) * B] = mm(allow, one_hot(z * QN + t), 1, 0).astype(BF16)

    def diagonal(s):
        rows = lax.broadcasted_iota(jnp.int32, (B, cols), 0) + (row * CN + s * YN + y) * B
        colid = lax.broadcasted_iota(jnp.int32, (B, cols), 1) + z * cols
        return rows == colid

    def mask_step(s, c):
        sb = row * CN + s * YN + y
        ok = mm(one_hot(sb), lang_cols[...], 0, 0)
        for t in range(QN):
            tile_ok = tile_ref[sb * B // TILE, (z * QN + t) * B // TILE]
            part = ok[:, t * B : (t + 1) * B]
            mask[s, :, t * B : (t + 1) * B] = jnp.where(tile_ok == 1, part, 0.0)
        return c

    lax.fori_loop(0, ZN, mask_step, 0)

    for d in range(1, JN):
        j = jpeer(d)
        t = slot(j, core)
        jwait(0, d, tun.at[t])
        cpush(0, j, tun.at[t], tun.at[t])
    if relays:
        pl.when(no(at_end))(across.wait_send)
        sends.append((across, at_end))
        zpush_to(0, opposite, sun.at[z], sun.at[z], no(at_end))
    for d in range(JN):
        j = jpeer(d)
        cwait(0, j, tun.at[slot(j, other)])

    colx[q] = jnp.zeros((1, cols), F32)

    def totals(s):
        diag = diagonal(s)
        sim = mm(sun[s], tun[...].reshape(cols, D), 1, 1)
        logits = SCALE * (sim - jnp.where(diag, MARGIN, 0.0))
        e = jnp.where(diag | (mask[s] > 0.5), jnp.exp(logits - SCALE), 0.0)
        e_ref[s] = e
        part = e[:, :LANES]
        for t in range(1, cols // LANES):
            part += e[:, t * LANES : (t + 1) * LANES]
        rowx[z, pl.ds(s, 1), :] = jnp.sum(part.T, axis=0, keepdims=True)
        colx[q] += jnp.sum(e, axis=0, keepdims=True)

    totals(z)
    if relays:
        s = scatter_c
        pl.when(no(at_end))(
            lambda: arrive(sun.at[s], zs_sem.at[0, s], zr_sem.at[0, s], zdev(s))
        )
        push(sun.at[s], sun.at[s], rs_sem.at[2], zr_sem.at[0, s], zdev(last - s), no(at_end))
        first = 1 + lax.rem(z, 2)
        final = last * (1 - z // 2)
        order = [first, last * 2 - z - first - final, final]
    else:
        order = [zpeer(d) for d in range(1, ZN)]

    def take(s):
        arrive(sun.at[s], zs_sem.at[0, 1], zr_sem.at[0, s], zdev(s))

    for k, s in enumerate(order):
        if relays and k == len(order) - 1:
            pl.when(no(middle(s)))(functools.partial(take, s))
        else:
            take(s)
        totals(s)
    for d in range(1, ZN):
        zpush(1, d, rowx.at[z], rowx.at[z])
    for d in range(1, QN):
        push(colx.at[q], colx.at[q], qs_sem.at[d], qr_sem.at[q], qdev(qpeer(d)))
    for d in range(1, ZN):
        zwait(1, d, rowx.at[zpeer(d)])
    for d in range(1, QN):
        t = qpeer(d)
        arrive(colx.at[t], qs_sem.at[d], qr_sem.at[t], qdev(t))
    row_inv[...] = (0.5 * SCALE) / jnp.sum(rowx[...], axis=0)
    col_inv = (0.5 * SCALE) / jnp.sum(colx[...], axis=0)

    def grad_block(s):
        inv = jnp.broadcast_to(row_inv[pl.ds(s, 1), :], (B, B)).T[:, :1]
        g = e_ref[s] * (inv + col_inv) - jnp.where(diagonal(s), SCALE, 0.0)
        g = g.astype(BF16)
        for t in range(QN):
            g_ref[t, pl.ds(pl.multiple_of(s * B, B), B), :] = g[:, t * B : (t + 1) * B]
        return mm(g, tun[...].reshape(cols, D), 1, 0)

    def split(part, unit):
        u = unit.astype(F32)
        along = jnp.sum(part * u, axis=-1, keepdims=True)
        rest = part - along * u
        return rest.astype(BF16), jnp.broadcast_to(along, (B, B)).T[:1, :]

    def along_unit(along, unit):
        return jnp.broadcast_to(along, (B, B)).T[:, :1] * unit.astype(F32)

    def source_part(s):
        part = grad_block(s)
        u = sun[s].astype(F32)
        along = jnp.sum(part * u, axis=-1, keepdims=True)
        return part - along * u, jnp.broadcast_to(along, (B, B)).T[:1, :]

    def send_sources(s, cond=None):
        zpush_to(2, s, ssend.at[s], srecv.at[z], cond)
        zpush_to(5, s, salong.at[s], ralong.at[z], cond)

    for s in (opposite, scatter_b, scatter_c) if relays else [zpeer(d) for d in range(1, ZN)]:
        rest, along = source_part(s)
        ssend[s] = rest.astype(BF16)
        salong[s] = along
        if not relays:
            send_sources(s)
        elif s is opposite:
            send_sources(s, no(at_end))
            by = zdev(z + 1 - 2 * lax.rem(z, 2))
            push(salong.at[s], passed_along, rs_sem.at[1], rr_sem.at[1], by, at_end)
            push(ssend.at[s], passed, rs_sem.at[0], rr_sem.at[0], by, at_end)
            to_pass, _ = sends.pop()
        elif s is scatter_b:
            send_sources(s, no(at_end))
        else:
            hold[...] = rest
            hold_along[...] = along
    src_grad = grad_block(z)

    def tgt_part(t):
        return mm(g_ref[t], sun[...].reshape(ZN * B, D), 0, 0)

    for d in range(1, JN + 1):
        j = jpeer(d)
        tcs[j] = tgt_part(slot(j, other))
        cpush(1, j, tcs.at[j], tcr.at[j])
    if relays:
        s = scatter_c

        @pl.when(no(at_end))
        def _():
            dev = zdev(opposite)
            arrive(passed, rs_sem.at[0], rr_sem.at[0], dev)
            arrive(passed_along, rs_sem.at[1], rr_sem.at[1], dev)
            ssend[s] = (hold[...] + passed[...].astype(F32)).astype(BF16)
            salong[s] = hold_along[...] + passed_along[...]

        pl.when(at_end)(to_pass.wait_send)
        send_sources(scatter_b, at_end)
        send_sources(s)
    for d in range(1, JN):
        j = jpeer(d)
        t = slot(j, core)
        part = tgt_part(t)
        cwait(1, j, tcr.at[j])
        rest, along = split(part + tcr[j], tun[t])
        tsend[j] = rest
        talong[j] = along
        jpush(1, d, tsend.at[j], trecv.at[jme])
        jpush(2, d, talong.at[j], qalong.at[jme])
    tgt_grad = tgt_part(q)
    cwait(1, jme, tcr.at[jme])
    tgt_grad += tcr[jme]

    def direction(raw, grad):
        r = raw[...]
        length = jnp.sqrt(jnp.sum(r * r, axis=-1, keepdims=True) + 1e-06)
        unit = r / length
        return (
            (grad - unit * jnp.sum(unit * grad, axis=-1, keepdims=True)) / length
        ).astype(BF16)

    along = jnp.zeros((1, B), F32)
    for d in range(1, JN):
        j = jpeer(d)
        jwait(1, d, trecv.at[j])
        jwait(2, d, qalong.at[j])
        tgt_grad += trecv[j].astype(F32)
        along += qalong[j]
    tgt_grad += along_unit(along, tun[q])
    tgt_dir = direction(traw, tgt_grad)
    w_ref[...] = mm(tgt_ref[...], tgt_dir, 0, 0)
    gtgt_ref[...] = mm(tgt_dir, proj_ref[...], 1, 1).astype(BF16)
    store(gtgt_ref, gtgt_hbm, loc_sem.at[5])

    src_acc[...] = src_grad
    along_acc[...] = jnp.zeros((1, B), F32)
    for d in range(1, ZN):
        s = zpeer(d)

        def add(d=d, s=s):
            zwait(2, d, srecv.at[s])
            zwait(5, d, ralong.at[s])
            src_acc[...] += srecv[s].astype(F32)
            along_acc[...] += ralong[s]

        if relays:
            pl.when(no(far(s)))(add)
        else:
            add()
    src_grad = src_acc[...] + along_unit(along_acc[...], sun[z])
    src_dir = direction(sraw, src_grad)

    w_ref[...] += mm(src_ref[...], src_dir, 0, 0)

    def rows_of(t):
        return pl.ds(pl.multiple_of(t * W, 16), W)

    for d in range(1, JN + 1):
        j = jpeer(d)
        wcs[j] = w_ref[rows_of(slot(j, other)), :].astype(BF16)
        cpush(2, j, wcs.at[j], wcr.at[j])
    gsrc_ref[...] = mm(src_dir, proj_ref[...], 1, 1).astype(BF16)
    store(gsrc_ref, gsrc_hbm, loc_sem.at[6])
    for d in range(1, JN):
        j = jpeer(d)
        cwait(2, j, wcr.at[j])
        wsend[j] = (w_ref[rows_of(slot(j, core)), :] + wcr[j].astype(F32)).astype(BF16)
        jpush(3, d, wsend.at[j], wrecv.at[jme])
    cwait(2, jme, wcr.at[jme])
    total = w_ref[rows_of(q), :] + wcr[jme].astype(F32)
    for d in range(1, JN):
        j = jpeer(d)
        jwait(3, d, wrecv.at[j])
        total += wrecv[j].astype(F32)
    for p in range(ZN):
        a, b = p // PC, p % PC
        zpart[p] = total[a * HR : (a + 1) * HR, b * HC : (b + 1) * HC]
    for d in range(1, ZN):
        s = zpeer(d)
        zsend[s] = zpart[s].astype(BF16)
        zpush(3, d, zsend.at[s], zrecv.at[z])
    piece = zpart[z]
    for d in range(1, ZN):
        s = zpeer(d)
        zwait(3, d, zrecv.at[s])
        piece += zrecv[s].astype(F32)
    wfin[q, z] = piece.astype(BF16)
    for d in range(1, ZN):
        zpush(4, d, wfin.at[q, z], wfin.at[q, z])

    def put(t, p):
        r = pl.ds(pl.multiple_of(t * W + (p // PC) * HR, 16), HR)
        c = pl.ds(pl.multiple_of(lax.rem(p, PC) * HC, LANES), HC)
        store(wfin.at[t, p], gproj_hbm.at[r, c], out_sem.at[t, p])

    for k in range(ZN):
        p = zpeer(k)
        if k:
            zwait(4, k, wfin.at[q, p])
        here = wfin.at[q, p]
        for d in range(1, JN):
            push(here, here, fs_sem.at[d, p], fr_sem.at[jme, p], jdev(jpeer(d)))
        push(here, here, hs_sem.at[jme, p], hr_sem.at[jme, p], sibling)
        put(q, p)
    for k in range(ZN):
        p = zpeer(k)
        for d in range(1, JN):
            j = jpeer(d)
            t = slot(j, core)
            here = wfin.at[t, p]
            arrive(here, fs_sem.at[d, p], fr_sem.at[j, p], jdev(j))
            push(here, here, hs_sem.at[j, p], hr_sem.at[j, p], sibling)
            put(t, p)
    for k in range(ZN):
        p = zpeer(k)
        for d in range(JN):
            j = jpeer(d)
            t = slot(j, other)
            arrive(wfin.at[t, p], hs_sem.at[j, p], hr_sem.at[j, p], sibling)
            put(t, p)
    for c, cond in sends:
        if cond is None:
            c.wait_send()
        else:
            pl.when(cond)(c.wait_send)
    for c in stores:
        c.wait()


def finish(gs_in, gt_in, gp_in, gs_out, gt_out, gp_out, low, wide, held, whole_sem, in_sem, out_sem):
    rows = low.shape[1]
    whole_in = [
        pltpu.make_async_copy(a, held.at[k], whole_sem.at[k]) for k, a in enumerate([gs_in, gt_in])
    ]
    whole_out = [
        pltpu.make_async_copy(held.at[k], b, whole_sem.at[2 + k])
        for k, b in enumerate([gs_out, gt_out])
    ]
    loads = [
        pltpu.make_async_copy(gp_in.at[pl.ds(k * rows, rows), :], low.at[k], in_sem.at[k])
        for k in range(PARTS)
    ]
    stores = [
        pltpu.make_async_copy(wide.at[k], gp_out.at[pl.ds(k * rows, rows), :], out_sem.at[k])
        for k in range(PARTS)
    ]
    for c in loads + whole_in:
        c.start()
    for k in range(PARTS):
        loads[k].wait()
        wide[k] = low[k].astype(F32)
        stores[k].start()
    for k in range(2):
        whole_in[k].wait()
        whole_out[k].start()
    for c in whole_out + stores:
        c.wait()


def fused_device(RN, CN, PR, PC, sources, targets, projection, language, lang_allow, tile_allow):
    ZN, QN, JN = CN // YN, RN * YN, RN * YN // CORES
    B, D = sources.shape
    NL = lang_allow.shape[0]
    W = D // QN
    langs = language.reshape(-1, B)
    smem = pl.BlockSpec(memory_space=pltpu.SMEM)
    hbm = pl.BlockSpec(memory_space=pltpu.HBM)
    V = pltpu.VMEM
    S = pltpu.SemaphoreType.DMA
    piece = (ZN, W // PR, D // PC)
    grad_sources, grad_targets, grad_proj = pl.pallas_call(
        functools.partial(fused, RN, ZN, PR, PC),
        out_shape=(
            jax.ShapeDtypeStruct((B, D), BF16),
            jax.ShapeDtypeStruct((B, D), BF16),
            jax.ShapeDtypeStruct((D, D), BF16),
        ),
        in_specs=[hbm] * 5 + [smem],
        out_specs=(hbm,) * 3,
        scratch_shapes=[
            V((B, D), BF16),
            V((B, D), BF16),
            V((D, D), BF16),
            V(langs.shape, jnp.int32),
            V((NL, NL), jnp.int32),
            V((B, D), BF16),
            V((B, D), BF16),
            V((B, D), F32),
            V((B, D), F32),
            V((ZN, B, D), BF16),
            V((QN, B, D), BF16),
            V((NL, QN * B), BF16),
            V((ZN, B, QN * B), F32),
            V((ZN, B, QN * B), F32),
            V((QN, ZN * B, B), BF16),
            V((ZN, ZN, B), F32),
            V((ZN, B), F32),
            V((QN, 1, QN * B), F32),
            V((ZN, B, D), BF16),
            V((ZN, B, D), BF16),
            V((JN, B, D), F32),
            V((JN, B, D), F32),
            V((JN, B, D), BF16),
            V((JN, B, D), BF16),
            V((ZN, 1, B), F32),
            V((ZN, 1, B), F32),
            V((JN, 1, B), F32),
            V((JN, 1, B), F32),
            V((D, D), F32),
            V((JN, W, D), BF16),
            V((JN, W, D), BF16),
            V((JN, W, D), BF16),
            V((JN, W, D), BF16),
            V(piece, F32),
            V(piece, BF16),
            V(piece, BF16),
            V((QN, *piece), BF16),
            S((7,)),
            S((6, ZN)),
            S((6, ZN)),
            S((QN,)),
            S((QN,)),
            S((4, JN)),
            S((4, JN)),
            S((3, JN)),
            S((3, JN)),
            S((JN, ZN)),
            S((JN, ZN)),
            S((JN, ZN)),
            S((JN, ZN)),
            S((QN, ZN)),
            V((B, D), F32),
            V((1, B), F32),
            V((B, D), BF16),
            V((1, B), F32),
            V((B, D), F32),
            V((1, B), F32),
            S((5,)),
            S((2,)),
        ],
        compiler_params=pltpu.CompilerParams(
            collective_id=0, has_side_effects=True, vmem_limit_bytes=60 * 2**20
        ),
    )(sources, targets, projection, langs, lang_allow, tile_allow)
    rows = D // PARTS
    return pl.pallas_call(
        finish,
        out_shape=(
            jax.ShapeDtypeStruct((B, D), BF16),
            jax.ShapeDtypeStruct((B, D), BF16),
            jax.ShapeDtypeStruct((D, D), F32),
        ),
        in_specs=[hbm] * 3,
        out_specs=(hbm,) * 3,
        scratch_shapes=[
            V((PARTS, rows, D), BF16),
            V((PARTS, rows, D), F32),
            V((2, B, D), BF16),
            S((4,)),
            S((PARTS,)),
            S((PARTS,)),
        ],
        compiler_params=pltpu.CompilerParams(vmem_limit_bytes=60 * 2**20),
    )(grad_sources, grad_targets, grad_proj)


def embedded(inputs, projection):
    raw_proj = jnp.dot(inputs, projection, preferred_element_type=jnp.float32)
    length = jnp.sqrt(jnp.sum(raw_proj * raw_proj, axis=-1, keepdims=True) + 1e-06)
    return (raw_proj, length)


def permitted(row_index, col_index, language, lang_allow, tile_allow):
    tile_cols = jnp.take(tile_allow, col_index // TILE, axis=1)
    tile_ok = jnp.take(tile_cols, row_index // TILE, axis=0)
    row_lang = lax.dynamic_slice_in_dim(language, row_index[0], row_index.shape[0])
    col_lang = lax.dynamic_slice_in_dim(language, col_index[0], col_index.shape[0])
    lang_cols = jnp.take(lang_allow, col_lang, axis=1)
    pair_ok = jnp.take(lang_cols, row_lang, axis=0)
    return (tile_ok * pair_ok == 1) | (row_index[:, None] == col_index[None, :])


def backward_proj(inputs, raw_proj, length, upstream, projection):
    unit_vec = raw_proj / length
    dir_grad = (
        (upstream - unit_vec * jnp.sum(unit_vec * upstream, axis=-1, keepdims=True)) / length
    ).astype(jnp.bfloat16)
    grad_in = jnp.dot(dir_grad, projection.T, preferred_element_type=jnp.float32).astype(
        jnp.bfloat16
    )
    grad_weight = jnp.dot(inputs.T, dir_grad, preferred_element_type=jnp.float32)
    return (grad_in, grad_weight)


def per_device(sources, targets, projection, language, lang_allow, tile_allow):
    src_raw, src_len = embedded(sources, projection)
    tgt_raw, tgt_len = embedded(targets, projection)
    src_unit = (src_raw / src_len).astype(jnp.bfloat16)
    tgt_unit = (tgt_raw / tgt_len).astype(jnp.bfloat16)
    row_emb = lax.all_gather(src_unit, "col", axis=0, tiled=True)
    col_emb = lax.all_gather(tgt_unit, "row", axis=0, tiled=True)
    row_count = row_emb.shape[0]
    col_count = col_emb.shape[0]
    row_begin = lax.axis_index("row") * row_count
    col_begin = lax.axis_index("col") * col_count
    row_index = row_begin + jnp.arange(row_count)
    col_index = col_begin + jnp.arange(col_count)
    allowed = permitted(row_index, col_index, language, lang_allow, tile_allow)
    similar = jnp.dot(row_emb, col_emb.T, preferred_element_type=jnp.float32)
    diagonal = (row_index[:, None] == col_index[None, :]).astype(jnp.float32)
    logits = SCALE * (similar - MARGIN * diagonal)
    weights = jnp.where(allowed, jnp.exp(logits - SCALE), jnp.float32(0.0))
    row_part = jnp.sum(weights, axis=1)
    col_part = jnp.sum(weights, axis=0)
    row_total = lax.psum(row_part, "col")
    col_total = lax.psum(col_part, "row")
    row_lse = jnp.log(row_total) + SCALE
    col_lse = jnp.log(col_total) + SCALE
    soft_rows = jnp.where(allowed, jnp.exp(logits - row_lse[:, None]), jnp.float32(0.0))
    soft_cols = jnp.where(allowed, jnp.exp(logits - col_lse[None, :]), jnp.float32(0.0))
    logit_grad = (SCALE * (0.5 * (soft_rows + soft_cols) - diagonal)).astype(jnp.bfloat16)
    src_terms = jnp.dot(logit_grad, col_emb, preferred_element_type=jnp.float32)
    src_grad = lax.psum_scatter(src_terms, "col", scatter_dimension=0, tiled=True)
    tgt_terms = lax.dot_general(
        logit_grad, row_emb, (((0,), (0,)), ((), ())), preferred_element_type=jnp.float32
    )
    tgt_grad = lax.psum_scatter(tgt_terms, "row", scatter_dimension=0, tiled=True)
    grad_sources, weight_src = backward_proj(sources, src_raw, src_len, src_grad, projection)
    grad_targets, weight_tgt = backward_proj(targets, tgt_raw, tgt_len, tgt_grad, projection)
    grad_proj = lax.psum(weight_src + weight_tgt, ("row", "col"))
    return (grad_sources, grad_targets, grad_proj)


def pieces(ZN, W, D):
    for PR in (1, 2, 4):
        if ZN % PR == 0 and W % (16 * PR) == 0 and D % (LANES * (ZN // PR)) == 0:
            return PR, ZN // PR
    return None


def solution(mesh):
    RN, CN = mesh.shape["row"], mesh.shape["col"]

    def device(sources, targets, projection, language, lang_allow, tile_allow):
        B, D = sources.shape
        split = None
        if CN % YN == 0 and RN % CORES == 0 and D % (16 * RN * YN) == 0 and B == LANES and RN * CN <= 64:
            split = pieces(CN // YN, D // (RN * YN), D)
        args = (sources, targets, projection, language, lang_allow, tile_allow)
        if split is None:
            return per_device(*args)
        return fused_device(RN, CN, *split, *args)

    return jax.shard_map(
        device,
        mesh=mesh,
        in_specs=(P(("row", "col"), None), P(("col", "row"), None), P(), P(), P(), P()),
        out_specs=(P(("row", "col"), None), P(("col", "row"), None), P()),
        check_vma=False,
    )
```
